256 devices in a mesh: ia: 8 (over z_lo, x), ja: 8 (over z_hi, core), ka: 4 (over y).
Axes of the slice: x: 4, y: 4, z: 8 (z_hi: 4, z_lo: 2; z = z_hi * 2 + z_lo), core: 2. Of those that a mesh axis runs over, the one named last changes fastest.
Arguments:
- tensor: bfloat16 [16384, 128, 512], P('ia', 'ja', 'ka'), may hold values from 0 to 8
- factor_b: bfloat16 [128, 64], P(('ja', 'ka')), may hold values from 0.049804688 to 1
- factor_c: bfloat16 [512, 64], P('ka'), may hold values from 0.049804688 to 1
- factor_a: float32 [16384, 64], P(('ia', 'ja', 'ka')), may hold values from 0 to 1
- restart: int32 [12], replicated, may hold values 0 or 1
Outputs:
- updated: float32 [16384, 64], P(('ia', 'ja', 'ka'))
- gram_a: float32 [64, 64], replicated
The draws below stay inside these ranges and needn't reach their ends.
All inputs are finite; a program needn't handle non-finite values.
Results may differ from the reference program's by a relative error of at most 0.0003.
Values may be sent and summed in bfloat16 or wider, within the bound.
A program may use at most 64 MiB of HBM per device.

```python
import jax
import jax.numpy as jnp
from jax import lax

R = 64
ITERS = 12
I = 16384
J = 128
K = 512


def touch_ends(result, stream_key, smallest, top_value):
    longest = result.shape.index(max(result.shape))
    spots = []
    for shift in (0, 1):
        where = [jax.random.randint(jax.random.fold_in(stream_key, axis), (), 0, length) for axis, length in enumerate(result.shape)]
        where[longest] = (where[longest] + shift) % result.shape[longest]
        spots.append(tuple(where))
    return result.at[spots[0]].set(smallest).at[spots[1]].set(top_value)


def levels(rng, shape, shards, smallest, high):
    gain = 1.0
    for axis_at, parts in shards:
        heights = jax.random.uniform(jax.random.fold_in(jax.random.fold_in(rng, 6), axis_at), (parts,), jnp.float32, smallest / len(shards), high / len(shards))
        gain = gain * jnp.repeat(jnp.exp(heights), shape[axis_at] // parts).reshape((-1,) + (1,) * (len(shape) - 1 - axis_at))
    return gain


def setup_inputs(seed: int = 0) -> dict:
    seeds = jax.random.split(jax.random.key(seed), 6)
    return {
        "tensor": jnp.clip(8.0 * jax.random.uniform(seeds[0], (I, J, K), jnp.float32) ** levels(seeds[0], (I, J, K), ((0, 8), (1, 8), (2, 4)), -0.2, 0.2), 0.0, 8.0).astype(jnp.bfloat16),
        "factor_b": jnp.clip(0.049804688 + 0.9501953 * jax.random.uniform(seeds[1], (J, R), jnp.float32) ** levels(seeds[1], (J, R), ((0, 32),), -0.2, 0.2), 0.049804688, 1.0).astype(jnp.bfloat16),
        "factor_c": jnp.clip(0.049804688 + 0.9501953 * jax.random.uniform(seeds[2], (K, R), jnp.float32) ** levels(seeds[2], (K, R), ((0, 4),), -0.2, 0.2), 0.049804688, 1.0).astype(jnp.bfloat16),
        "factor_a": jnp.clip(1.0 * jax.random.uniform(seeds[3], (I, R), jnp.float32) ** levels(seeds[3], (I, R), ((0, 256),), -0.2, 0.2), 0.0, 1.0),
        "restart": touch_ends((jax.random.randint(seeds[4], (ITERS,), 0, 2) < 1).astype(jnp.int32), jax.random.fold_in(seeds[4], 1), 0, 1),
    }


def reference(tensor, factor_b, factor_c, factor_a, restart):
    rows, cols, depth = tensor.shape
    partial_value = jnp.dot(tensor.reshape(rows * cols, depth), factor_c, preferred_element_type=jnp.float32).reshape(rows, cols, R)
    mttkrp = lax.optimization_barrier(jnp.sum(partial_value * factor_b.astype(jnp.float32)[None, :, :], axis=1))
    gram_b = jnp.dot(factor_b.T, factor_b, preferred_element_type=jnp.float32)
    gram_c = jnp.dot(factor_c.T, factor_c, preferred_element_type=jnp.float32)
    gram = gram_b * gram_c
    lip = jnp.sqrt(jnp.sum(gram * gram))
    current = factor_a
    look = factor_a
    tval = jnp.float32(1.0)
    for step in range(ITERS):
        flag = restart[step].astype(jnp.float32)
        look = flag * current + (1.0 - flag) * look
        tval = flag + (1.0 - flag) * tval
        grad = jnp.dot(look, gram, precision=lax.Precision.HIGHEST) - mttkrp
        nxt = jnp.maximum(look - grad / lip, 0.0)
        t_next = (1.0 + jnp.sqrt(1.0 + 4.0 * tval * tval)) / 2.0
        look = nxt + (tval - 1.0) / t_next * (nxt - current)
        current = nxt
        tval = t_next
    gram_a = jnp.dot(current.T, current, precision=lax.Precision.HIGHEST)
    return (current, gram_a)
```

```python
import functools

import jax
import jax.numpy as jnp
from jax import lax
from jax.experimental import pallas as pl
from jax.experimental.pallas import tpu as pltpu
from jax.sharding import PartitionSpec as P

ITERS = 12
MESH = pl.DeviceIdType.MESH
BLOCKS = 32
HALF = 32


def far_first(n):
    return 2 + n - (n // 2) * (2 * n - 1)


def add_rows(stack, row):
    for bit in (1, 2, 4):
        keep = (row & bit) == 0
        stack = [
            jnp.where(keep, u, v) + pltpu.roll(jnp.where(keep, v, u), 8 - bit, 0)
            for u, v in zip(stack[0::2], stack[1::2])
        ]
    return stack[0]


def split(value):
    high = value.astype(jnp.bfloat16)
    return high, (value - high.astype(jnp.float32)).astype(jnp.bfloat16)


def kernel(
    t_hbm, b_hbm, ct_hbm, a_hbm, restart_hbm, up_ref, gram_ref,
    t_ref, prod, b_in, ct_in, a_in, flags,
    b_slots, b_block, b_all, ct_all, weight_c,
    give, got, mine, out_rs, in_rs, weight_g, coef,
    gram_out, gram_z, gram_half, gram_xy,
    t_sem, in_sem, b_s, b_r, c_s, c_r, ball_s, ball_r,
    x_s, x_r, rs_s, rs_r, z_s, z_r, xy_s, xy_r,
):
    f32, bf16 = jnp.float32, jnp.bfloat16
    ia, ja, y = lax.axis_index("ia"), lax.axis_index("ja"), lax.axis_index("ka")
    z_lo, x, z_hi, core = ia // 4, ia % 4, ja // 2, ja % 2
    z = z_hi * 2 + z_lo

    def device(z, x, y, core):
        return ((z % 2) * 4 + x, (z // 2) * 2 + core, y)

    def remote(src, dst, send, recv, to):
        return pltpu.make_async_remote_copy(
            src_ref=src, dst_ref=dst, send_sem=send, recv_sem=recv, device_id=to, device_id_type=MESH
        )

    loads = [
        pltpu.make_async_copy(b_hbm, b_in, in_sem.at[0]),
        pltpu.make_async_copy(ct_hbm, ct_in, in_sem.at[1]),
        pltpu.make_async_copy(a_hbm, a_in, in_sem.at[2]),
        pltpu.make_async_copy(restart_hbm, flags, in_sem.at[3]),
    ]
    for load in loads:
        load.start()

    def tensor_load(n):
        return pltpu.make_async_copy(t_hbm.at[pl.ds(n * 64, 64)], t_ref.at[n], t_sem.at[n])

    @pl.loop(0, BLOCKS)
    def _(n):
        tensor_load(n).start()

    barrier = pltpu.get_barrier_semaphore()

    def greet(to):
        pl.semaphore_signal(barrier, inc=1, device_id=to, device_id_type=MESH)

    @pl.loop(1, 32)
    def _(n):
        greet(device((z + 2 * (n // 8)) % 8, x, (y + (n // 2) % 4) % 4, (core + n % 2) % 2))

    @pl.loop(0, 8)
    def _(n):
        greet(device((z + 1 + 2 * (n // 2)) % 8, x, y, n % 2))

    @pl.loop(0, 24)
    def _(n):
        greet(device(z, (x + 1 + n // 8) % 4, (n // 2) % 4, n % 2))

    for load in loads:
        load.wait()
    ct = ct_in[...]
    wide_c = ct.astype(f32).T.astype(bf16)
    zero = jnp.zeros((128, 64), bf16)
    weight_c[...] = jnp.concatenate(
        [jnp.concatenate([wide_c, zero], 1), jnp.concatenate([zero, wide_c], 1)], 0
    )
    ct_all[y] = jnp.concatenate([ct, ct], 0)
    b_own = b_in[...].astype(f32)
    b_slots[y, 0:4, :] = jnp.concatenate([b_own, b_own], 1)

    def block_product(n):
        tensor_load(n).wait()
        rows = t_ref[n]
        left = rows[:HALF].reshape(HALF * 16, 128)
        right = rows[HALF:].reshape(HALF * 16, 128)
        prod[n] = jnp.dot(jnp.concatenate([left, right], 1), weight_c[...], preferred_element_type=f32)

    @pl.loop(0, BLOCKS // 2)
    def _(n):
        block_product(n)

    pl.semaphore_wait(barrier, 63)

    def b_copy(n):
        to = (y + n) % 4
        return remote(b_slots.at[y], b_slots.at[y], b_s.at[n], b_r.at[n], device(z, x, to, core))

    def c_copy(n):
        to = (y + n) % 4
        return remote(ct_all.at[y], ct_all.at[y], c_s.at[n], c_r.at[n], device(z, x, to, core))

    for n in (2, 1, 3):
        b_copy(n).start()
    for n in (2, 1, 3):
        c_copy(n).start()

    @pl.loop(BLOCKS // 2, BLOCKS)
    def _(n):
        block_product(n)

    for n in (2, 1, 3):
        b_copy(n).wait()
    for part in range(4):
        b_block[4 * part : 4 * part + 4, :] = b_slots[part, 0:4, :]
    b_all[ja] = b_block[...].astype(bf16)

    row = lax.broadcasted_iota(jnp.int32, (8, 128), 0)

    def target(n):
        return (z_hi + far_first(n // 4)) % 4, (y + far_first(n % 4)) % 4

    def block_sum(n, at_core, out):
        to_z, to_y = target(n)
        block = (to_z * 2 + at_core) * 4 + to_y
        low, high = b_block[0:8, :], b_block[8:16, :]
        for group in range(HALF // 8):
            stack = []
            for pair in range(8):
                start = (group * 8 + pair) * 16
                stack.append(
                    prod[block, start : start + 8, :] * low + prod[block, start + 8 : start + 16, :] * high
                )
            out[n, group * 8 : group * 8 + 8, :] = add_rows(stack, row)

    def core_copy(n):
        return remote(give.at[n], got.at[n], x_s.at[n], x_r.at[n], device(z, x, y, 1 - core))

    @pl.loop(0, 16)
    def _(n):
        block_sum(n, 1 - core, give)
        core_copy(n).start()

    @pl.loop(0, 16)
    def _(n):
        block_sum(n, core, mine)

    def plane_copy(n):
        to_z, to_y = target(n)
        return remote(out_rs.at[n], in_rs.at[n], rs_s.at[n], rs_r.at[n], device(to_z * 2 + z_lo, x, to_y, core))

    @pl.loop(0, 15)
    def _(n):
        core_copy(n).wait()
        out_rs[n] = mine[n] + got[n]
        plane_copy(n).start()

    def ball_copy(n):
        to = (ja + n) % 8
        return remote(
            b_all.at[ja], b_all.at[ja], ball_s.at[n], ball_r.at[n], device((to // 2) * 2 + z_lo, x, y, to % 2)
        )

    for n in range(1, 8):
        ball_copy(n).start()

    for n in (2, 1, 3):
        c_copy(n).wait()
    for n in range(1, 8):
        ball_copy(n).wait()
    b_rows = b_all[...].reshape(128, 128)
    gram_b = lax.dot_general(b_rows, b_rows, (((0,), (0,)), ((), ())), preferred_element_type=f32)
    gram_c = jnp.zeros((128, 128), f32)
    for part in range(4):
        piece = ct_all[part]
        gram_c += lax.dot_general(piece, piece, (((1,), (1,)), ((), ())), preferred_element_type=f32)
    rows2 = lax.broadcasted_iota(jnp.int32, (128, 128), 0)
    cols2 = lax.broadcasted_iota(jnp.int32, (128, 128), 1)
    gram = jnp.where((rows2 < 64) == (cols2 < 64), gram_b * gram_c, 0.0)
    lip = jnp.sqrt(0.5 * jnp.sum(jnp.sum(gram * gram, axis=0, keepdims=True), axis=1, keepdims=True))
    high, low = split(gram / lip)
    both = jnp.concatenate([high, low], 1)
    weight_g[...] = jnp.concatenate([both, both], 0)
    inverse = 1.0 / lip

    tval = jnp.ones((8, 128), f32)
    for step in range(ITERS):
        flag = flags[step].astype(f32)
        tval = flag + (1.0 - flag) * tval
        t_next = (1.0 + jnp.sqrt(1.0 + 4.0 * tval * tval)) / 2.0
        coef[step] = (tval - 1.0) / t_next
        tval = t_next

    start = a_in[...]
    current = jnp.concatenate([start[:HALF], start[HALF:]], 1)

    core_copy(15).wait()
    total = mine[15] + got[15]
    for n in range(15):
        plane_copy(n).wait_recv()
        total = total + in_rs[n]
    target_term = total * inverse

    look = current
    weights = weight_g[...]
    for step in range(ITERS):
        flag = flags[step].astype(f32)
        look = flag * current + (1.0 - flag) * look
        high, low = split(look)
        wide = jnp.dot(jnp.concatenate([high, low], 1), weights, preferred_element_type=f32)
        grad = wide[:, :128] + wide[:, 128:] - target_term
        nxt = jnp.maximum(look - grad, 0.0)
        look = nxt + coef[step, 0:1, :] * (nxt - current)
        current = nxt

    turned = pltpu.roll(current, 64, 1)
    high, low = split(jnp.concatenate([current, turned], 0))
    gram_a = lax.dot_general(
        jnp.concatenate([high, low, high], 0),
        jnp.concatenate([high, high, low], 0),
        (((0,), (0,)), ((), ())),
        preferred_element_type=f32,
    )
    lane = lax.broadcasted_iota(jnp.int32, (HALF, 128), 1)
    packed = jnp.where(lane < 64, gram_a[0:32], gram_a[96:128])
    gram_out[0] = packed[:16]
    gram_out[1] = packed[16:]

    def z_peer(n):
        return (z + 4 + n // 2) % 8, (core + n % 2) % 2

    def z_copy(n):
        to_z, to_core = z_peer(n)
        return remote(gram_out.at[to_core], gram_z.at[core, z], z_s.at[n], z_r.at[n], device(to_z, x, y, to_core))

    for n in range(16):
        if n != 8:
            z_copy(n).start()
    gram_z[core, z] = gram_out[core]
    up_ref[0:HALF, :] = current[:, :64]
    up_ref[HALF:, :] = current[:, 64:]
    for n in range(16):
        if n != 8:
            z_copy(n).wait_recv()
    half = gram_z[0, 0]
    for n in range(1, 16):
        half = half + gram_z[n // 8, n % 8]
    gram_half[...] = half

    def xy_copy(n):
        to_x, to_y = (x + far_first(n // 8)) % 4, (y + far_first((n // 2) % 4)) % 4
        to_core = (core + n % 2) % 2
        return remote(
            gram_half, gram_xy.at[core, x * 4 + y], xy_s.at[n], xy_r.at[n], device(z, to_x, to_y, to_core)
        )

    for n in range(32):
        if n != 30:
            xy_copy(n).start()
    gram_xy[core, x * 4 + y] = half
    for n in range(32):
        if n != 30:
            xy_copy(n).wait_recv()
    for part in range(2):
        whole = gram_xy[part, 0]
        for n in range(1, 16):
            whole = whole + gram_xy[part, n]
        gram_ref[16 * part : 16 * part + 16, :] = whole[:, :64]
        gram_ref[HALF + 16 * part : HALF + 16 * part + 16, :] = whole[:, 64:]

    @pl.loop(0, 15)
    def _(n):
        plane_copy(n).wait_send()

    for n in range(16):
        if n != 8:
            z_copy(n).wait_send()
    for n in range(32):
        if n != 30:
            xy_copy(n).wait_send()


def shards(tensor, factor_b, factor_c, factor_a, restart):
    f32, bf16 = jnp.float32, jnp.bfloat16
    dma = pltpu.SemaphoreType.DMA
    return pl.pallas_call(
        kernel,
        out_shape=(
            jax.ShapeDtypeStruct((64, 64), f32),
            jax.ShapeDtypeStruct((64, 64), f32),
        ),
        in_specs=[pl.BlockSpec(memory_space=pl.ANY)] * 5,
        out_specs=[pl.BlockSpec(memory_space=pltpu.VMEM)] * 2,
        scratch_shapes=[
            pltpu.VMEM((BLOCKS, 64, 16, 128), bf16),
            pltpu.VMEM((BLOCKS, 512, 128), f32),
            pltpu.VMEM((4, 64), bf16),
            pltpu.VMEM((64, 128), bf16),
            pltpu.VMEM((64, 64), f32),
            pltpu.SMEM((ITERS,), jnp.int32),
            pltpu.VMEM((4, 8, 128), f32),
            pltpu.VMEM((16, 128), f32),
            pltpu.VMEM((8, 16, 128), bf16),
            pltpu.VMEM((4, 128, 128), bf16),
            pltpu.VMEM((256, 128), bf16),
            pltpu.VMEM((16, HALF, 128), f32),
            pltpu.VMEM((16, HALF, 128), f32),
            pltpu.VMEM((16, HALF, 128), f32),
            pltpu.VMEM((16, HALF, 128), f32),
            pltpu.VMEM((16, HALF, 128), f32),
            pltpu.VMEM((256, 256), bf16),
            pltpu.VMEM((ITERS, 8, 128), f32),
            pltpu.VMEM((2, 16, 128), f32),
            pltpu.VMEM((2, 8, 16, 128), f32),
            pltpu.VMEM((16, 128), f32),
            pltpu.VMEM((2, 16, 16, 128), f32),
            dma((BLOCKS,)), dma((4,)), dma((4,)), dma((4,)), dma((4,)), dma((4,)), dma((8,)), dma((8,)),
            dma((16,)), dma((16,)), dma((16,)), dma((16,)), dma((16,)), dma((16,)), dma((32,)), dma((32,)),
        ],
        compiler_params=pltpu.CompilerParams(
            collective_id=0, has_side_effects=True, vmem_limit_bytes=56 * 2**20
        ),
        name="cp_update",
    )(tensor, factor_b, factor_c.T, factor_a, restart)


def solution(mesh):
    return jax.shard_map(
        shards,
        mesh=mesh,
        in_specs=(
            P("ia", "ja", "ka"),
            P(("ja", "ka"), None),
            P("ka", None),
            P(("ia", "ja", "ka"), None),
            P(),
        ),
        out_specs=(P(("ia", "ja", "ka"), None), P()),
        check_vma=False,
    )
```

```python
import functools

import jax
import jax.numpy as jnp
from jax import lax
from jax.experimental import pallas as pl
from jax.experimental.pallas import tpu as pltpu
from jax.sharding import PartitionSpec as P

ITERS = 12
MESH = pl.DeviceIdType.MESH
BLOCKS = 32
GROUP = 8
HALF = 32

B, C, B_ALL, CORE, PLANE, Z, XY, KINDS = range(8)


def far_first(n):
    return 2 + n - (n // 2) * (2 * n - 1)


def add_rows(stack, row):
    for bit in (1, 2, 4):
        keep = (row & bit) == 0
        stack = [
            jnp.where(keep, u, v) + pltpu.roll(jnp.where(keep, v, u), 8 - bit, 0)
            for u, v in zip(stack[0::2], stack[1::2])
        ]
    return stack[0]


def split(value):
    high = value.astype(jnp.bfloat16)
    return high, (value - high.astype(jnp.float32)).astype(jnp.bfloat16)


def kernel(
    t_hbm, b_hbm, ct_hbm, a_hbm, restart_hbm, up_ref, gram_ref,
    t_ref, prod, b_in, ct_in, a_in, flags,
    b_slots, b_block, b_all, ct_all, weight_c,
    give, got, mine, out_rs, in_rs, weight_g, coef,
    gram_out, gram_z, gram_half, gram_xy,
    t_sem, in_sem, core_r, sent, got_all,
):
    f32, bf16 = jnp.float32, jnp.bfloat16
    ia, ja, y = lax.axis_index("ia"), lax.axis_index("ja"), lax.axis_index("ka")
    z_lo, x, z_hi, core = ia // 4, ia % 4, ja // 2, ja % 2
    z = z_hi * 2 + z_lo

    def device(z, x, y, core):
        return ((z % 2) * 4 + x, (z // 2) * 2 + core, y)

    def remote(src, dst, send, recv, to):
        return pltpu.make_async_remote_copy(
            src_ref=src, dst_ref=dst, send_sem=send, recv_sem=recv, device_id=to, device_id_type=MESH
        )

    def exchange(ref, kind):
        return remote(ref, ref, sent.at[kind], got_all.at[kind], device(z, x, y, 1 - core))

    loads = [
        pltpu.make_async_copy(b_hbm, b_in, in_sem.at[0]),
        pltpu.make_async_copy(ct_hbm, ct_in, in_sem.at[1]),
        pltpu.make_async_copy(a_hbm, a_in, in_sem.at[2]),
        pltpu.make_async_copy(restart_hbm, flags, in_sem.at[3]),
    ]
    for load in loads:
        load.start()

    def tensor_load(n):
        rows = pl.ds(n * GROUP * 64, GROUP * 64)
        return pltpu.make_async_copy(t_hbm.at[rows], t_ref.at[rows], t_sem.at[n])

    for n in range(BLOCKS // GROUP):
        tensor_load(n).start(priority=n % 2)

    barrier = pltpu.get_barrier_semaphore()

    def greet(to):
        pl.semaphore_signal(barrier, inc=1, device_id=to, device_id_type=MESH)

    @pl.loop(1, 32)
    def _(n):
        greet(device((z + 2 * (n // 8)) % 8, x, (y + (n // 2) % 4) % 4, (core + n % 2) % 2))

    @pl.loop(0, 8)
    def _(n):
        greet(device((z + 1 + 2 * (n // 2)) % 8, x, y, n % 2))

    @pl.loop(0, 24)
    def _(n):
        greet(device(z, (x + 1 + n // 8) % 4, (n // 2) % 4, n % 2))

    for load in loads:
        load.wait()
    ct = ct_in[...]
    wide_c = ct.astype(f32).T.astype(bf16)
    zero = jnp.zeros((128, 64), bf16)
    weight_c[...] = jnp.concatenate(
        [jnp.concatenate([wide_c, zero], 1), jnp.concatenate([zero, wide_c], 1)], 0
    )
    ct_all[y] = jnp.concatenate([ct, ct], 0)
    b_own = b_in[...].astype(f32)
    b_slots[y, 0:4, :] = jnp.concatenate([b_own, b_own], 1)

    def product(n):
        tensor_load(n).wait()
        rows = t_ref[pl.ds(n * GROUP * 64, GROUP * 64)].reshape(GROUP, 64, 16, 128)
        left = rows[:, :HALF].reshape(GROUP * HALF * 16, 128)
        right = rows[:, HALF:].reshape(GROUP * HALF * 16, 128)
        out = jnp.dot(jnp.concatenate([left, right], 1), weight_c[...], preferred_element_type=f32)
        prod[pl.ds(n * GROUP, GROUP)] = out.reshape(GROUP, HALF * 16, 128)

    @pl.loop(0, BLOCKS // GROUP - 1)
    def _(n):
        product(n)

    pl.semaphore_wait(barrier, 63)

    def b_copy(n):
        to = (y + n) % 4
        return remote(b_slots.at[y], b_slots.at[y], sent.at[B], got_all.at[B], device(z, x, to, core))

    def c_copy(n):
        to = (y + n) % 4
        return remote(ct_all.at[y], ct_all.at[y], sent.at[C], got_all.at[C], device(z, x, to, core))

    for n in (2, 1, 3):
        b_copy(n).start()
    for n in (2, 1, 3):
        c_copy(n).start()

    product(BLOCKS // GROUP - 1)

    exchange(b_slots.at[0:3], B).wait()
    for part in range(4):
        b_block[4 * part : 4 * part + 4, :] = b_slots[part, 0:4, :]
    b_all[ja] = b_block[...].astype(bf16)

    row = lax.broadcasted_iota(jnp.int32, (8, 128), 0)

    def target(n):
        return (z_hi + far_first(n // 4)) % 4, (y + far_first(n % 4)) % 4

    def block_sum(n, at_core, out):
        to_z, to_y = target(n)
        block = (to_z * 2 + at_core) * 4 + to_y
        low, high = b_block[0:8, :], b_block[8:16, :]
        for group in range(HALF // 8):
            stack = []
            for pair in range(8):
                start = (group * 8 + pair) * 16
                stack.append(
                    prod[block, start : start + 8, :] * low + prod[block, start + 8 : start + 16, :] * high
                )
            out[n, group * 8 : group * 8 + 8, :] = add_rows(stack, row)

    def core_copy(n):
        return remote(give.at[n], got.at[n], sent.at[CORE], core_r.at[n // 4], device(z, x, y, 1 - core))

    @pl.loop(0, 16)
    def _(n):
        block_sum(n, 1 - core, give)
        core_copy(n).start()

    @pl.loop(0, 16)
    def _(n):
        block_sum(n, core, mine)

    def plane_copy(n):
        to_z, to_y = target(n)
        return remote(
            out_rs.at[n], in_rs.at[n], sent.at[PLANE], got_all.at[PLANE], device(to_z * 2 + z_lo, x, to_y, core)
        )

    for part in range(4):
        blocks = got.at[4 * part : 4 * part + 4]
        remote(blocks, blocks, sent.at[CORE], core_r.at[part], device(z, x, y, 1 - core)).wait_recv()

        @pl.loop(4 * part, min(4 * part + 4, 15))
        def _(n):
            out_rs[n] = mine[n] + got[n]
            plane_copy(n).start()

    def ball_copy(n):
        to = (ja + n) % 8
        return remote(
            b_all.at[ja], b_all.at[ja], sent.at[B_ALL], got_all.at[B_ALL], device((to // 2) * 2 + z_lo, x, y, to % 2)
        )

    for n in range(1, 8):
        ball_copy(n).start()

    exchange(ct_all.at[0:3], C).wait()
    exchange(b_all.at[0:7], B_ALL).wait()
    b_rows = b_all[...].reshape(128, 128)
    gram_b = lax.dot_general(b_rows, b_rows, (((0,), (0,)), ((), ())), preferred_element_type=f32)
    gram_c = jnp.zeros((128, 128), f32)
    for part in range(4):
        piece = ct_all[part]
        gram_c += lax.dot_general(piece, piece, (((1,), (1,)), ((), ())), preferred_element_type=f32)
    rows2 = lax.broadcasted_iota(jnp.int32, (128, 128), 0)
    cols2 = lax.broadcasted_iota(jnp.int32, (128, 128), 1)
    gram = jnp.where((rows2 < 64) == (cols2 < 64), gram_b * gram_c, 0.0)
    lip = jnp.sqrt(0.5 * jnp.sum(jnp.sum(gram * gram, axis=0, keepdims=True), axis=1, keepdims=True))
    high, low = split(gram / lip)
    both = jnp.concatenate([high, low], 1)
    weight_g[...] = jnp.concatenate([both, both], 0)
    inverse = 1.0 / lip

    tval = jnp.ones((8, 128), f32)
    for step in range(ITERS):
        flag = flags[step].astype(f32)
        tval = flag + (1.0 - flag) * tval
        t_next = (1.0 + jnp.sqrt(1.0 + 4.0 * tval * tval)) / 2.0
        coef[step] = (tval - 1.0) / t_next
        tval = t_next

    start = a_in[...]
    current = jnp.concatenate([start[:HALF], start[HALF:]], 1)

    total = mine[15] + got[15]
    exchange(in_rs.at[0:15], PLANE).wait_recv()
    for n in range(15):
        total = total + in_rs[n]
    target_term = total * inverse

    look = current
    weights = weight_g[...]
    for step in range(ITERS):
        flag = flags[step].astype(f32)
        look = flag * current + (1.0 - flag) * look
        high, low = split(look)
        wide = jnp.dot(jnp.concatenate([high, low], 1), weights, preferred_element_type=f32)
        grad = wide[:, :128] + wide[:, 128:] - target_term
        nxt = jnp.maximum(look - grad, 0.0)
        look = nxt + coef[step, 0:1, :] * (nxt - current)
        current = nxt

    turned = pltpu.roll(current, 64, 1)
    high, low = split(jnp.concatenate([current, turned], 0))
    gram_a = lax.dot_general(
        jnp.concatenate([high, low, high], 0),
        jnp.concatenate([high, high, low], 0),
        (((0,), (0,)), ((), ())),
        preferred_element_type=f32,
    )
    lane = lax.broadcasted_iota(jnp.int32, (HALF, 128), 1)
    packed = jnp.where(lane < 64, gram_a[0:32], gram_a[96:128])
    gram_out[0] = packed[:16]
    gram_out[1] = packed[16:]

    def z_peer(n):
        step = (4, 3, 5, 2, 6, 1, 7, 0)[n // 2]
        return (z + step) % 8, (core + n % 2) % 2

    def z_copy(n):
        to_z, to_core = z_peer(n)
        return remote(
            gram_out.at[to_core], gram_z.at[core * 8 + z], sent.at[Z], got_all.at[Z], device(to_z, x, y, to_core)
        )

    for n in range(16):
        if n != 14:
            z_copy(n).start()
    gram_z[core * 8 + z] = gram_out[core]
    up_ref[0:HALF, :] = current[:, :64]
    up_ref[HALF:, :] = current[:, 64:]
    exchange(gram_z.at[0:15], Z).wait_recv()
    half = gram_z[0]
    for n in range(1, 16):
        half = half + gram_z[n]
    gram_half[...] = half

    def xy_copy(n):
        step = (10, 11, 9, 14, 6, 8, 2, 15, 13, 7, 5, 12, 4, 3, 1, 0)[n // 2]
        to_x, to_y = (x + step // 4) % 4, (y + step % 4) % 4
        to_core = (core + n % 2) % 2
        return remote(
            gram_half, gram_xy.at[core * 16 + x * 4 + y], sent.at[XY], got_all.at[XY], device(z, to_x, to_y, to_core)
        )

    for n in range(32):
        if n != 30:
            xy_copy(n).start()
    gram_xy[core * 16 + x * 4 + y] = half
    exchange(gram_xy.at[0:31], XY).wait_recv()
    for part in range(2):
        whole = gram_xy[16 * part]
        for n in range(1, 16):
            whole = whole + gram_xy[16 * part + n]
        gram_ref[16 * part : 16 * part + 16, :] = whole[:, :64]
        gram_ref[HALF + 16 * part : HALF + 16 * part + 16, :] = whole[:, 64:]

    exchange(give, CORE).wait_send()
    exchange(out_rs.at[0:15], PLANE).wait_send()
    exchange(gram_z.at[0:15], Z).wait_send()
    exchange(gram_xy.at[0:31], XY).wait_send()


def write_out(up_ref, gram_ref, up_hbm, gram_hbm, sem):
    copies = [
        pltpu.make_async_copy(up_ref, up_hbm, sem.at[0]),
        pltpu.make_async_copy(gram_ref, gram_hbm, sem.at[1]),
    ]
    for copy in copies:
        copy.start()
    for copy in copies:
        copy.wait()


def shards(tensor, factor_b, factor_c, factor_a, restart):
    f32, bf16 = jnp.float32, jnp.bfloat16
    dma = pltpu.SemaphoreType.DMA
    result = jax.ShapeDtypeStruct((64, 64), f32)
    operands = [
        pltpu.with_memory_space_constraint(array, pltpu.HBM)
        for array in (tensor, factor_b, factor_c.T, factor_a, restart)
    ]
    updated, gram_a = pl.pallas_call(
        kernel,
        out_shape=(pltpu.VMEM((64, 64), f32), pltpu.VMEM((64, 64), f32)),
        in_specs=[pl.BlockSpec(memory_space=pltpu.HBM)] * 5,
        out_specs=[pl.BlockSpec(memory_space=pltpu.VMEM)] * 2,
        scratch_shapes=[
            pltpu.VMEM((BLOCKS * 64, 16, 128), bf16),
            pltpu.VMEM((BLOCKS, 512, 128), f32),
            pltpu.VMEM((4, 64), bf16),
            pltpu.VMEM((64, 128), bf16),
            pltpu.VMEM((64, 64), f32),
            pltpu.SMEM((ITERS,), jnp.int32),
            pltpu.VMEM((4, 8, 128), f32),
            pltpu.VMEM((16, 128), f32),
            pltpu.VMEM((8, 16, 128), bf16),
            pltpu.VMEM((4, 128, 128), bf16),
            pltpu.VMEM((256, 128), bf16),
            pltpu.VMEM((16, HALF, 128), f32),
            pltpu.VMEM((16, HALF, 128), f32),
            pltpu.VMEM((16, HALF, 128), f32),
            pltpu.VMEM((16, HALF, 128), f32),
            pltpu.VMEM((16, HALF, 128), f32),
            pltpu.VMEM((256, 256), bf16),
            pltpu.VMEM((ITERS, 8, 128), f32),
            pltpu.VMEM((2, 16, 128), f32),
            pltpu.VMEM((16, 16, 128), f32),
            pltpu.VMEM((16, 128), f32),
            pltpu.VMEM((32, 16, 128), f32),
            dma((BLOCKS // GROUP,)), dma((4,)), dma((4,)), dma((KINDS,)), dma((KINDS,)),
        ],
        compiler_params=pltpu.CompilerParams(
            collective_id=0, has_side_effects=True, vmem_limit_bytes=32 * 2**20
        ),
        name="cp_update",
    )(*operands)
    return pl.pallas_call(
        write_out,
        out_shape=(result, result),
        in_specs=[pl.BlockSpec(memory_space=pltpu.VMEM)] * 2,
        out_specs=[pl.BlockSpec(memory_space=pltpu.HBM)] * 2,
        scratch_shapes=[dma((2,))],
        name="write_out",
    )(*(pltpu.with_memory_space_constraint(array, pltpu.VMEM) for array in (updated, gram_a)))


def solution(mesh):
    return jax.shard_map(
        shards,
        mesh=mesh,
        in_specs=(
            P("ia", "ja", "ka"),
            P(("ja", "ka"), None),
            P("ka", None),
            P(("ia", "ja", "ka"), None),
            P(),
        ),
        out_specs=(P(("ia", "ja", "ka"), None), P()),
        check_vma=False,
    )
```

```python
import functools

import jax
import jax.numpy as jnp
from jax import lax
from jax.experimental import pallas as pl
from jax.experimental.pallas import tpu as pltpu
from jax.sharding import PartitionSpec as P

ITERS = 12
MESH = pl.DeviceIdType.MESH
BLOCKS = 32
GROUP = 8
HALF = 32
OFFSET = 32767
STEPS = 2.0 * OFFSET
B, C, B_ALL, CORE, PLANE, PLANE_STEP, Z, XY, KINDS = range(9)


def far_first(n):
    return 2 + n - (n // 2) * (2 * n - 1)


def add_rows(stack, row):
    for bit in (1, 2, 4):
        keep = (row & bit) == 0
        stack = [
            jnp.where(keep, u, v) + pltpu.roll(jnp.where(keep, v, u), 8 - bit, 0)
            for u, v in zip(stack[0::2], stack[1::2])
        ]
    return stack[0]


def encode(value):
    top = jnp.maximum(jnp.max(value, axis=0, keepdims=True), 2e-34)
    codes = (value * (STEPS / top) + 0.5).astype(jnp.int32) - OFFSET
    return codes.astype(jnp.int16), top * (1.0 / STEPS)


def decode(codes, step):
    return (codes.astype(jnp.int32).astype(jnp.float32) + OFFSET) * step


def split(value):
    high = value.astype(jnp.bfloat16)
    return high, (value - high.astype(jnp.float32)).astype(jnp.bfloat16)


def kernel(
    t_hbm, b_hbm, ct_hbm, a_hbm, restart_hbm, up_ref, gram_ref,
    t_ref, prod, b_in, ct_in, a_in, flags,
    b_slots, b_block, b_all, ct_all, weight_c,
    give, got, mine, out_rs, in_rs, out_step, in_step, weight_g, coef,
    gram_out, gram_z, gram_half, gram_xy,
    t_sem, in_sem, core_r, sent, got_all,
):
    f32, bf16 = jnp.float32, jnp.bfloat16
    ia, ja, y = lax.axis_index("ia"), lax.axis_index("ja"), lax.axis_index("ka")
    z_lo, x, z_hi, core = ia // 4, ia % 4, ja // 2, ja % 2
    z = z_hi * 2 + z_lo

    def device(z, x, y, core):
        return ((z % 2) * 4 + x, (z // 2) * 2 + core, y)

    def remote(src, dst, send, recv, to):
        return pltpu.make_async_remote_copy(
            src_ref=src, dst_ref=dst, send_sem=send, recv_sem=recv, device_id=to, device_id_type=MESH
        )

    def exchange(ref, kind):
        return remote(ref, ref, sent.at[kind], got_all.at[kind], device(z, x, y, 1 - core))

    loads = [
        pltpu.make_async_copy(b_hbm, b_in, in_sem.at[0]),
        pltpu.make_async_copy(ct_hbm, ct_in, in_sem.at[1]),
        pltpu.make_async_copy(a_hbm, a_in, in_sem.at[2]),
        pltpu.make_async_copy(restart_hbm, flags, in_sem.at[3]),
    ]
    for load in loads:
        load.start()

    def tensor_load(n):
        rows = pl.ds(n * GROUP * 64, GROUP * 64)
        return pltpu.make_async_copy(t_hbm.at[rows], t_ref.at[rows], t_sem.at[n])

    for n in range(BLOCKS // GROUP):
        tensor_load(n).start(priority=n % 2)

    barrier = pltpu.get_barrier_semaphore()

    def greet(to):
        pl.semaphore_signal(barrier, inc=1, device_id=to, device_id_type=MESH)

    @pl.loop(1, 32)
    def _(n):
        greet(device((z + 2 * (n // 8)) % 8, x, (y + (n // 2) % 4) % 4, (core + n % 2) % 2))

    @pl.loop(0, 8)
    def _(n):
        greet(device((z + 1 + 2 * (n // 2)) % 8, x, y, n % 2))

    @pl.loop(0, 24)
    def _(n):
        greet(device(z, (x + 1 + n // 8) % 4, (n // 2) % 4, n % 2))

    for load in loads:
        load.wait()
    ct = ct_in[...]
    wide_c = ct.astype(f32).T.astype(bf16)
    zero = jnp.zeros((128, 64), bf16)
    weight_c[...] = jnp.concatenate(
        [jnp.concatenate([wide_c, zero], 1), jnp.concatenate([zero, wide_c], 1)], 0
    )
    ct_all[y] = jnp.concatenate([ct, ct], 0)
    b_own = b_in[...].astype(f32)
    b_slots[y, 0:4, :] = jnp.concatenate([b_own, b_own], 1)

    def product(n):
        tensor_load(n).wait()
        rows = t_ref[pl.ds(n * GROUP * 64, GROUP * 64)].reshape(GROUP, 64, 16, 128)
        left = rows[:, :HALF].reshape(GROUP * HALF * 16, 128)
        right = rows[:, HALF:].reshape(GROUP * HALF * 16, 128)
        out = jnp.dot(jnp.concatenate([left, right], 1), weight_c[...], preferred_element_type=f32)
        prod[pl.ds(n * GROUP, GROUP)] = out.reshape(GROUP, HALF * 16, 128)


    pl.semaphore_wait(barrier, 63)

    def b_copy(n):
        to = (y + n) % 4
        return remote(b_slots.at[y], b_slots.at[y], sent.at[B], got_all.at[B], device(z, x, to, core))

    def c_copy(n):
        to = (y + n) % 4
        return remote(ct_all.at[y], ct_all.at[y], sent.at[C], got_all.at[C], device(z, x, to, core))

    for n in (2, 1, 3):
        b_copy(n).start()
    for n in (2, 1, 3):
        c_copy(n).start()

    @pl.loop(0, BLOCKS // GROUP)
    def _(n):
        product(n)

    exchange(b_slots.at[0:3], B).wait()
    for part in range(4):
        b_block[4 * part : 4 * part + 4, :] = b_slots[part, 0:4, :]
    b_all[ja] = b_block[...].astype(bf16)

    row = lax.broadcasted_iota(jnp.int32, (8, 128), 0)

    def target(n):
        return (z_hi + far_first(n // 4)) % 4, (y + far_first(n % 4)) % 4

    def block_sum(n, at_core, out):
        to_z, to_y = target(n)
        block = (to_z * 2 + at_core) * 4 + to_y
        low, high = b_block[0:8, :], b_block[8:16, :]
        for group in range(HALF // 8):
            stack = []
            for pair in range(8):
                start = (group * 8 + pair) * 16
                stack.append(
                    prod[block, start : start + 8, :] * low + prod[block, start + 8 : start + 16, :] * high
                )
            out[n, group * 8 : group * 8 + 8, :] = add_rows(stack, row)

    def core_copy(n):
        return remote(give.at[n], got.at[n], sent.at[CORE], core_r.at[n // 4], device(z, x, y, 1 - core))

    @pl.loop(0, 16)
    def _(n):
        block_sum(n, 1 - core, give)
        core_copy(n).start()

    @pl.loop(0, 16)
    def _(n):
        block_sum(n, core, mine)

    def plane_copy(n, src, dst, kind):
        to_z, to_y = target(n)
        return remote(src.at[n], dst.at[n], sent.at[kind], got_all.at[kind], device(to_z * 2 + z_lo, x, to_y, core))

    for part in range(4):
        blocks = got.at[4 * part : 4 * part + 4]
        remote(blocks, blocks, sent.at[CORE], core_r.at[part], device(z, x, y, 1 - core)).wait_recv()

        @pl.loop(4 * part, min(4 * part + 4, 15))
        def _(n):
            out_rs[n], out_step[n] = encode(mine[n] + got[n])
            plane_copy(n, out_rs, in_rs, PLANE).start()
            plane_copy(n, out_step, in_step, PLANE_STEP).start()

    def ball_copy(n):
        to = (ja + n) % 8
        return remote(
            b_all.at[ja], b_all.at[ja], sent.at[B_ALL], got_all.at[B_ALL], device((to // 2) * 2 + z_lo, x, y, to % 2)
        )

    for n in range(1, 8):
        ball_copy(n).start()

    exchange(ct_all.at[0:3], C).wait()
    exchange(b_all.at[0:7], B_ALL).wait()
    b_rows = b_all[...].reshape(128, 128)
    gram_b = lax.dot_general(b_rows, b_rows, (((0,), (0,)), ((), ())), preferred_element_type=f32)
    gram_c = jnp.zeros((128, 128), f32)
    for part in range(4):
        piece = ct_all[part]
        gram_c += lax.dot_general(piece, piece, (((1,), (1,)), ((), ())), preferred_element_type=f32)
    rows2 = lax.broadcasted_iota(jnp.int32, (128, 128), 0)
    cols2 = lax.broadcasted_iota(jnp.int32, (128, 128), 1)
    gram = jnp.where((rows2 < 64) == (cols2 < 64), gram_b * gram_c, 0.0)
    lip = jnp.sqrt(0.5 * jnp.sum(jnp.sum(gram * gram, axis=0, keepdims=True), axis=1, keepdims=True))
    high, low = split(gram / lip)
    both = jnp.concatenate([high, low], 1)
    weight_g[...] = jnp.concatenate([both, both], 0)
    inverse = 1.0 / lip

    tval = jnp.ones((8, 128), f32)
    for step in range(ITERS):
        flag = flags[step].astype(f32)
        tval = flag + (1.0 - flag) * tval
        t_next = (1.0 + jnp.sqrt(1.0 + 4.0 * tval * tval)) / 2.0
        coef[step] = (tval - 1.0) / t_next
        tval = t_next

    start = a_in[...]
    current = jnp.concatenate([start[:HALF], start[HALF:]], 1)

    total = mine[15] + got[15]
    exchange(in_step.at[0:15], PLANE_STEP).wait_recv()
    exchange(in_rs.at[0:15], PLANE).wait_recv()
    for n in range(15):
        total = total + decode(in_rs[n], in_step[n])
    target_term = total * inverse

    look = current
    weights = weight_g[...]
    for step in range(ITERS):
        flag = flags[step].astype(f32)
        look = flag * current + (1.0 - flag) * look
        high, low = split(look)
        wide = jnp.dot(jnp.concatenate([high, low], 1), weights, preferred_element_type=f32)
        grad = wide[:, :128] + wide[:, 128:] - target_term
        nxt = jnp.maximum(look - grad, 0.0)
        look = nxt + coef[step, 0:1, :] * (nxt - current)
        current = nxt

    turned = pltpu.roll(current, 64, 1)
    high, low = split(jnp.concatenate([current, turned], 0))
    gram_a = lax.dot_general(
        jnp.concatenate([high, low, high], 0),
        jnp.concatenate([high, high, low], 0),
        (((0,), (0,)), ((), ())),
        preferred_element_type=f32,
    )
    lane = lax.broadcasted_iota(jnp.int32, (HALF, 128), 1)
    packed = jnp.where(lane < 64, gram_a[0:32], gram_a[96:128])
    gram_out[0] = packed[:16]
    gram_out[1] = packed[16:]

    def z_peer(n):
        step = (4, 3, 5, 2, 6, 1, 7, 0)[n // 2]
        return (z + step) % 8, (core + n % 2) % 2

    def z_copy(n):
        to_z, to_core = z_peer(n)
        return remote(
            gram_out.at[to_core], gram_z.at[core * 8 + z], sent.at[Z], got_all.at[Z], device(to_z, x, y, to_core)
        )

    for n in range(16):
        if n != 14:
            z_copy(n).start()
    gram_z[core * 8 + z] = gram_out[core]
    up_ref[0:HALF, :] = current[:, :64]
    up_ref[HALF:, :] = current[:, 64:]
    exchange(gram_z.at[0:15], Z).wait_recv()
    half = gram_z[0]
    for n in range(1, 16):
        half = half + gram_z[n]
    gram_half[...] = half

    def xy_copy(n):
        step = (10, 11, 9, 14, 6, 8, 2, 15, 13, 7, 5, 12, 4, 3, 1, 0)[n // 2]
        to_x, to_y = (x + step // 4) % 4, (y + step % 4) % 4
        to_core = (core + n % 2) % 2
        return remote(
            gram_half, gram_xy.at[core * 16 + x * 4 + y], sent.at[XY], got_all.at[XY], device(z, to_x, to_y, to_core)
        )

    for n in range(32):
        if n != 30:
            xy_copy(n).start()
    gram_xy[core * 16 + x * 4 + y] = half
    exchange(gram_xy.at[0:31], XY).wait_recv()
    for part in range(2):
        whole = gram_xy[16 * part]
        for n in range(1, 16):
            whole = whole + gram_xy[16 * part + n]
        gram_ref[16 * part : 16 * part + 16, :] = whole[:, :64]
        gram_ref[HALF + 16 * part : HALF + 16 * part + 16, :] = whole[:, 64:]

    exchange(give, CORE).wait_send()
    exchange(out_rs.at[0:15], PLANE).wait_send()
    exchange(out_step.at[0:15], PLANE_STEP).wait_send()
    exchange(gram_z.at[0:15], Z).wait_send()
    exchange(gram_xy.at[0:31], XY).wait_send()


def write_out(up_ref, gram_ref, up_hbm, gram_hbm, sem):
    copies = [
        pltpu.make_async_copy(up_ref, up_hbm, sem.at[0]),
        pltpu.make_async_copy(gram_ref, gram_hbm, sem.at[1]),
    ]
    for copy in copies:
        copy.start()
    for copy in copies:
        copy.wait()


def shards(tensor, factor_b, factor_c, factor_a, restart):
    f32, bf16 = jnp.float32, jnp.bfloat16
    dma = pltpu.SemaphoreType.DMA
    result = jax.ShapeDtypeStruct((64, 64), f32)
    operands = [
        pltpu.with_memory_space_constraint(array, pltpu.HBM)
        for array in (tensor, factor_b, factor_c.T, factor_a, restart)
    ]
    updated, gram_a = pl.pallas_call(
        kernel,
        out_shape=(pltpu.VMEM((64, 64), f32), pltpu.VMEM((64, 64), f32)),
        in_specs=[pl.BlockSpec(memory_space=pltpu.HBM)] * 5,
        out_specs=[pl.BlockSpec(memory_space=pltpu.VMEM)] * 2,
        scratch_shapes=[
            pltpu.VMEM((BLOCKS * 64, 16, 128), bf16),
            pltpu.VMEM((BLOCKS, 512, 128), f32),
            pltpu.VMEM((4, 64), bf16),
            pltpu.VMEM((64, 128), bf16),
            pltpu.VMEM((64, 64), f32),
            pltpu.SMEM((ITERS,), jnp.int32),
            pltpu.VMEM((4, 8, 128), f32),
            pltpu.VMEM((16, 128), f32),
            pltpu.VMEM((8, 16, 128), bf16),
            pltpu.VMEM((4, 128, 128), bf16),
            pltpu.VMEM((256, 128), bf16),
            pltpu.VMEM((16, HALF, 128), f32),
            pltpu.VMEM((16, HALF, 128), f32),
            pltpu.VMEM((16, HALF, 128), f32),
            pltpu.VMEM((16, HALF, 128), jnp.int16),
            pltpu.VMEM((16, HALF, 128), jnp.int16),
            pltpu.VMEM((16, 1, 128), f32),
            pltpu.VMEM((16, 1, 128), f32),
            pltpu.VMEM((256, 256), bf16),
            pltpu.VMEM((ITERS, 8, 128), f32),
            pltpu.VMEM((2, 16, 128), f32),
            pltpu.VMEM((16, 16, 128), f32),
            pltpu.VMEM((16, 128), f32),
            pltpu.VMEM((32, 16, 128), f32),
            dma((BLOCKS // GROUP,)), dma((4,)), dma((4,)), dma((KINDS,)), dma((KINDS,)),
        ],
        compiler_params=pltpu.CompilerParams(
            collective_id=0, has_side_effects=True, vmem_limit_bytes=32 * 2**20
        ),
        name="cp_update",
    )(*operands)
    return pl.pallas_call(
        write_out,
        out_shape=(result, result),
        in_specs=[pl.BlockSpec(memory_space=pltpu.VMEM)] * 2,
        out_specs=[pl.BlockSpec(memory_space=pltpu.HBM)] * 2,
        scratch_shapes=[dma((2,))],
        name="write_out",
    )(*(pltpu.with_memory_space_constraint(array, pltpu.VMEM) for array in (updated, gram_a)))


def solution(mesh):
    return jax.shard_map(
        shards,
        mesh=mesh,
        in_specs=(
            P("ia", "ja", "ka"),
            P(("ja", "ka"), None),
            P("ka", None),
            P(("ia", "ja", "ka"), None),
            P(),
        ),
        out_specs=(P(("ia", "ja", "ka"), None), P()),
        check_vma=False,
    )
```

```python
import functools

import jax
import jax.numpy as jnp
from jax import lax
from jax.experimental import pallas as pl
from jax.experimental.pallas import tpu as pltpu
from jax.sharding import PartitionSpec as P

ITERS = 12
MESH = pl.DeviceIdType.MESH
BLOCKS = 32
GROUP = 8
HALF = 32
OFFSET = 32767
STEPS = 2.0 * OFFSET
B, C, B_ALL, CORE, PLANE, PLANE_STEP, Z, Z_STEP, XY, XY_STEP, KINDS = range(11)


def far_first(n):
    return 2 + n - (n // 2) * (2 * n - 1)


def add_rows(stack, row):
    for bit in (1, 2, 4):
        keep = (row & bit) == 0
        stack = [
            jnp.where(keep, u, v) + pltpu.roll(jnp.where(keep, v, u), 8 - bit, 0)
            for u, v in zip(stack[0::2], stack[1::2])
        ]
    return stack[0]


def encode(value):
    top = jnp.maximum(jnp.max(value, axis=0, keepdims=True), 2e-34)
    codes = (value * (STEPS / top) + 0.5).astype(jnp.int32) - OFFSET
    return codes.astype(jnp.int16), top * (1.0 / STEPS)


def decode(codes, step):
    return (codes.astype(jnp.int32).astype(jnp.float32) + OFFSET) * step


def split(value):
    high = value.astype(jnp.bfloat16)
    return high, (value - high.astype(jnp.float32)).astype(jnp.bfloat16)


def kernel(
    t_hbm, b_hbm, ct_hbm, a_hbm, restart_hbm, up_ref, gram_ref,
    t_ref, prod, b_in, ct_in, a_in, flags,
    b_slots, b_block, b_all, ct_all, weight_c,
    give, got, mine, out_rs, in_rs, out_step, in_step, weight_g, coef,
    gram_out, gram_z, gram_half, gram_xy,
    gram_step, gram_z_step, half_step, gram_xy_step,
    t_sem, in_sem, core_r, sent, got_all,
):
    f32, bf16 = jnp.float32, jnp.bfloat16
    ia, ja, y = lax.axis_index("ia"), lax.axis_index("ja"), lax.axis_index("ka")
    z_lo, x, z_hi, core = ia // 4, ia % 4, ja // 2, ja % 2
    z = z_hi * 2 + z_lo

    def device(z, x, y, core):
        return ((z % 2) * 4 + x, (z // 2) * 2 + core, y)

    def remote(src, dst, send, recv, to):
        return pltpu.make_async_remote_copy(
            src_ref=src, dst_ref=dst, send_sem=send, recv_sem=recv, device_id=to, device_id_type=MESH
        )

    def exchange(ref, kind):
        return remote(ref, ref, sent.at[kind], got_all.at[kind], device(z, x, y, 1 - core))

    loads = [
        pltpu.make_async_copy(b_hbm, b_in, in_sem.at[0]),
        pltpu.make_async_copy(ct_hbm, ct_in, in_sem.at[1]),
        pltpu.make_async_copy(a_hbm, a_in, in_sem.at[2]),
        pltpu.make_async_copy(restart_hbm, flags, in_sem.at[3]),
    ]
    for load in loads:
        load.start()

    def tensor_load(n):
        rows = pl.ds(n * GROUP * 64, GROUP * 64)
        return pltpu.make_async_copy(t_hbm.at[rows], t_ref.at[rows], t_sem.at[n])

    for n in range(BLOCKS // GROUP):
        tensor_load(n).start(priority=n % 2)

    barrier = pltpu.get_barrier_semaphore()

    def greet(to):
        pl.semaphore_signal(barrier, inc=1, device_id=to, device_id_type=MESH)

    @pl.loop(1, 32)
    def _(n):
        greet(device((z + 2 * (n // 8)) % 8, x, (y + (n // 2) % 4) % 4, (core + n % 2) % 2))

    @pl.loop(0, 8)
    def _(n):
        greet(device((z + 1 + 2 * (n // 2)) % 8, x, y, n % 2))

    @pl.loop(0, 24)
    def _(n):
        greet(device(z, (x + 1 + n // 8) % 4, (n // 2) % 4, n % 2))

    for load in loads:
        load.wait()
    ct = ct_in[...]
    wide_c = ct.astype(f32).T.astype(bf16)
    zero = jnp.zeros((128, 64), bf16)
    weight_c[...] = jnp.concatenate(
        [jnp.concatenate([wide_c, zero], 1), jnp.concatenate([zero, wide_c], 1)], 0
    )
    ct_all[y] = jnp.concatenate([ct, ct], 0)
    b_own = b_in[...].astype(f32)
    b_slots[y, 0:4, :] = jnp.concatenate([b_own, b_own], 1)

    def product(n):
        tensor_load(n).wait()
        rows = t_ref[pl.ds(n * GROUP * 64, GROUP * 64)].reshape(GROUP, 64, 16, 128)
        left = rows[:, :HALF].reshape(GROUP * HALF * 16, 128)
        right = rows[:, HALF:].reshape(GROUP * HALF * 16, 128)
        out = jnp.dot(jnp.concatenate([left, right], 1), weight_c[...], preferred_element_type=f32)
        prod[pl.ds(n * GROUP, GROUP)] = out.reshape(GROUP, HALF * 16, 128)


    pl.semaphore_wait(barrier, 63)

    def b_copy(n):
        to = (y + n) % 4
        return remote(b_slots.at[y], b_slots.at[y], sent.at[B], got_all.at[B], device(z, x, to, core))

    def c_copy(n):
        to = (y + n) % 4
        return remote(ct_all.at[y], ct_all.at[y], sent.at[C], got_all.at[C], device(z, x, to, core))

    for n in (2, 1, 3):
        b_copy(n).start()
    for n in (2, 1, 3):
        c_copy(n).start()

    @pl.loop(0, BLOCKS // GROUP)
    def _(n):
        product(n)

    exchange(b_slots.at[0:3], B).wait()
    for part in range(4):
        b_block[4 * part : 4 * part + 4, :] = b_slots[part, 0:4, :]
    b_all[ja] = b_block[...].astype(bf16)

    row = lax.broadcasted_iota(jnp.int32, (8, 128), 0)

    def target(n):
        return (z_hi + far_first(n // 4)) % 4, (y + far_first(n % 4)) % 4

    def block_sum(n, at_core, out):
        to_z, to_y = target(n)
        block = (to_z * 2 + at_core) * 4 + to_y
        low, high = b_block[0:8, :], b_block[8:16, :]
        for group in range(HALF // 8):
            stack = []
            for pair in range(8):
                start = (group * 8 + pair) * 16
                stack.append(
                    prod[block, start : start + 8, :] * low + prod[block, start + 8 : start + 16, :] * high
                )
            out[n, group * 8 : group * 8 + 8, :] = add_rows(stack, row)

    def core_copy(n):
        return remote(give.at[n], got.at[n], sent.at[CORE], core_r.at[n // 4], device(z, x, y, 1 - core))

    @pl.loop(0, 16)
    def _(n):
        block_sum(n, 1 - core, give)
        core_copy(n).start()

    @pl.loop(0, 16)
    def _(n):
        block_sum(n, core, mine)

    def plane_copy(n, src, dst, kind):
        to_z, to_y = target(n)
        return remote(src.at[n], dst.at[n], sent.at[kind], got_all.at[kind], device(to_z * 2 + z_lo, x, to_y, core))

    for part in range(4):
        blocks = got.at[4 * part : 4 * part + 4]
        remote(blocks, blocks, sent.at[CORE], core_r.at[part], device(z, x, y, 1 - core)).wait_recv()

        @pl.loop(4 * part, min(4 * part + 4, 15))
        def _(n):
            out_rs[n], out_step[n] = encode(mine[n] + got[n])
            plane_copy(n, out_rs, in_rs, PLANE).start()
            plane_copy(n, out_step, in_step, PLANE_STEP).start()

    def ball_copy(n):
        to = (ja + n) % 8
        return remote(
            b_all.at[ja], b_all.at[ja], sent.at[B_ALL], got_all.at[B_ALL], device((to // 2) * 2 + z_lo, x, y, to % 2)
        )

    for n in range(1, 8):
        ball_copy(n).start()

    exchange(ct_all.at[0:3], C).wait()
    exchange(b_all.at[0:7], B_ALL).wait()
    b_rows = b_all[...].reshape(128, 128)
    gram_b = lax.dot_general(b_rows, b_rows, (((0,), (0,)), ((), ())), preferred_element_type=f32)
    gram_c = jnp.zeros((128, 128), f32)
    for part in range(4):
        piece = ct_all[part]
        gram_c += lax.dot_general(piece, piece, (((1,), (1,)), ((), ())), preferred_element_type=f32)
    rows2 = lax.broadcasted_iota(jnp.int32, (128, 128), 0)
    cols2 = lax.broadcasted_iota(jnp.int32, (128, 128), 1)
    gram = jnp.where((rows2 < 64) == (cols2 < 64), gram_b * gram_c, 0.0)
    lip = jnp.sqrt(0.5 * jnp.sum(jnp.sum(gram * gram, axis=0, keepdims=True), axis=1, keepdims=True))
    high, low = split(gram / lip)
    both = jnp.concatenate([high, low], 1)
    weight_g[...] = jnp.concatenate([both, both], 0)
    inverse = 1.0 / lip

    tval = jnp.ones((8, 128), f32)
    for step in range(ITERS):
        flag = flags[step].astype(f32)
        tval = flag + (1.0 - flag) * tval
        t_next = (1.0 + jnp.sqrt(1.0 + 4.0 * tval * tval)) / 2.0
        coef[step] = (tval - 1.0) / t_next
        tval = t_next

    start = a_in[...]
    current = jnp.concatenate([start[:HALF], start[HALF:]], 1)

    total = mine[15] + got[15]
    exchange(in_step.at[0:15], PLANE_STEP).wait_recv()
    exchange(in_rs.at[0:15], PLANE).wait_recv()
    for n in range(15):
        total = total + decode(in_rs[n], in_step[n])
    target_term = total * inverse

    look = current
    weights = weight_g[...]
    for step in range(ITERS):
        flag = flags[step].astype(f32)
        look = flag * current + (1.0 - flag) * look
        high, low = split(look)
        wide = jnp.dot(jnp.concatenate([high, low], 1), weights, preferred_element_type=f32)
        grad = wide[:, :128] + wide[:, 128:] - target_term
        nxt = jnp.maximum(look - grad, 0.0)
        look = nxt + coef[step, 0:1, :] * (nxt - current)
        current = nxt

    turned = pltpu.roll(current, 64, 1)
    high, low = split(jnp.concatenate([current, turned], 0))
    gram_a = lax.dot_general(
        jnp.concatenate([high, low, high], 0),
        jnp.concatenate([high, high, low], 0),
        (((0,), (0,)), ((), ())),
        preferred_element_type=f32,
    )
    lane = lax.broadcasted_iota(jnp.int32, (HALF, 128), 1)
    packed = jnp.where(lane < 64, gram_a[0:32], gram_a[96:128])
    gram_out[0], gram_step[0] = encode(packed[:16])
    gram_out[1], gram_step[1] = encode(packed[16:])

    def z_peer(n):
        step = (4, 3, 5, 2, 6, 1, 7, 0)[n // 2]
        return (z + step) % 8, (core + n % 2) % 2

    def z_copy(n, src, dst, kind):
        to_z, to_core = z_peer(n)
        return remote(
            src.at[to_core], dst.at[core * 8 + z], sent.at[kind], got_all.at[kind], device(to_z, x, y, to_core)
        )

    for n in range(16):
        if n != 14:
            z_copy(n, gram_out, gram_z, Z).start()
            z_copy(n, gram_step, gram_z_step, Z_STEP).start()
    gram_z[core * 8 + z] = gram_out[core]
    gram_z_step[core * 8 + z] = gram_step[core]
    up_ref[0:HALF, :] = current[:, :64]
    up_ref[HALF:, :] = current[:, 64:]
    exchange(gram_z.at[0:15], Z).wait_recv()
    exchange(gram_z_step.at[0:15], Z_STEP).wait_recv()
    half = decode(gram_z[0], gram_z_step[0])
    for n in range(1, 16):
        half = half + decode(gram_z[n], gram_z_step[n])
    gram_half[...], half_step[...] = encode(half)

    def xy_copy(n, src, dst, kind):
        step = (10, 11, 9, 14, 6, 8, 2, 15, 13, 7, 5, 12, 4, 3, 1, 0)[n // 2]
        to_x, to_y = (x + step // 4) % 4, (y + step % 4) % 4
        to_core = (core + n % 2) % 2
        return remote(
            src, dst.at[core * 16 + x * 4 + y], sent.at[kind], got_all.at[kind], device(z, to_x, to_y, to_core)
        )

    for n in range(32):
        if n != 30:
            xy_copy(n, gram_half, gram_xy, XY).start()
            xy_copy(n, half_step, gram_xy_step, XY_STEP).start()
    gram_xy[core * 16 + x * 4 + y] = gram_half[...]
    gram_xy_step[core * 16 + x * 4 + y] = half_step[...]
    exchange(gram_xy.at[0:31], XY).wait_recv()
    exchange(gram_xy_step.at[0:31], XY_STEP).wait_recv()
    for part in range(2):
        whole = decode(gram_xy[16 * part], gram_xy_step[16 * part])
        for n in range(1, 16):
            whole = whole + decode(gram_xy[16 * part + n], gram_xy_step[16 * part + n])
        gram_ref[16 * part : 16 * part + 16, :] = whole[:, :64]
        gram_ref[HALF + 16 * part : HALF + 16 * part + 16, :] = whole[:, 64:]

    exchange(give, CORE).wait_send()
    exchange(out_rs.at[0:15], PLANE).wait_send()
    exchange(out_step.at[0:15], PLANE_STEP).wait_send()
    exchange(gram_z.at[0:15], Z).wait_send()
    exchange(gram_z_step.at[0:15], Z_STEP).wait_send()
    exchange(gram_xy.at[0:31], XY).wait_send()
    exchange(gram_xy_step.at[0:31], XY_STEP).wait_send()


def write_out(up_ref, gram_ref, up_hbm, gram_hbm, sem):
    copies = [
        pltpu.make_async_copy(up_ref, up_hbm, sem.at[0]),
        pltpu.make_async_copy(gram_ref, gram_hbm, sem.at[1]),
    ]
    for copy in copies:
        copy.start()
    for copy in copies:
        copy.wait()


def shards(tensor, factor_b, factor_c, factor_a, restart):
    f32, bf16 = jnp.float32, jnp.bfloat16
    dma = pltpu.SemaphoreType.DMA
    result = jax.ShapeDtypeStruct((64, 64), f32)
    operands = [
        pltpu.with_memory_space_constraint(array, pltpu.HBM)
        for array in (tensor, factor_b, factor_c.T, factor_a, restart)
    ]
    updated, gram_a = pl.pallas_call(
        kernel,
        out_shape=(pltpu.VMEM((64, 64), f32), pltpu.VMEM((64, 64), f32)),
        in_specs=[pl.BlockSpec(memory_space=pltpu.HBM)] * 5,
        out_specs=[pl.BlockSpec(memory_space=pltpu.VMEM)] * 2,
        scratch_shapes=[
            pltpu.VMEM((BLOCKS * 64, 16, 128), bf16),
            pltpu.VMEM((BLOCKS, 512, 128), f32),
            pltpu.VMEM((4, 64), bf16),
            pltpu.VMEM((64, 128), bf16),
            pltpu.VMEM((64, 64), f32),
            pltpu.SMEM((ITERS,), jnp.int32),
            pltpu.VMEM((4, 8, 128), f32),
            pltpu.VMEM((16, 128), f32),
            pltpu.VMEM((8, 16, 128), bf16),
            pltpu.VMEM((4, 128, 128), bf16),
            pltpu.VMEM((256, 128), bf16),
            pltpu.VMEM((16, HALF, 128), f32),
            pltpu.VMEM((16, HALF, 128), f32),
            pltpu.VMEM((16, HALF, 128), f32),
            pltpu.VMEM((16, HALF, 128), jnp.int16),
            pltpu.VMEM((16, HALF, 128), jnp.int16),
            pltpu.VMEM((16, 1, 128), f32),
            pltpu.VMEM((16, 1, 128), f32),
            pltpu.VMEM((256, 256), bf16),
            pltpu.VMEM((ITERS, 8, 128), f32),
            pltpu.VMEM((2, 16, 128), jnp.int16),
            pltpu.VMEM((16, 16, 128), jnp.int16),
            pltpu.VMEM((16, 128), jnp.int16),
            pltpu.VMEM((32, 16, 128), jnp.int16),
            pltpu.VMEM((2, 1, 128), f32),
            pltpu.VMEM((16, 1, 128), f32),
            pltpu.VMEM((1, 128), f32),
            pltpu.VMEM((32, 1, 128), f32),
            dma((BLOCKS // GROUP,)), dma((4,)), dma((4,)), dma((KINDS,)), dma((KINDS,)),
        ],
        compiler_params=pltpu.CompilerParams(
            collective_id=0, has_side_effects=True, vmem_limit_bytes=32 * 2**20
        ),
        name="cp_update",
    )(*operands)
    return pl.pallas_call(
        write_out,
        out_shape=(result, result),
        in_specs=[pl.BlockSpec(memory_space=pltpu.VMEM)] * 2,
        out_specs=[pl.BlockSpec(memory_space=pltpu.HBM)] * 2,
        scratch_shapes=[dma((2,))],
        name="write_out",
    )(*(pltpu.with_memory_space_constraint(array, pltpu.VMEM) for array in (updated, gram_a)))


def solution(mesh):
    return jax.shard_map(
        shards,
        mesh=mesh,
        in_specs=(
            P("ia", "ja", "ka"),
            P(("ja", "ka"), None),
            P("ka", None),
            P(("ia", "ja", "ka"), None),
            P(),
        ),
        out_specs=(P(("ia", "ja", "ka"), None), P()),
        check_vma=False,
    )
```

```python
import functools

import jax
import jax.numpy as jnp
from jax import lax
from jax.experimental import pallas as pl
from jax.experimental.pallas import tpu as pltpu
from jax.sharding import PartitionSpec as P

ITERS = 12
MESH = pl.DeviceIdType.MESH
BLOCKS = 32
GROUP = 8
HALF = 32
OFFSET = 32767
STEPS = 2.0 * OFFSET
B, C, B_ALL, CORE, PLANE, PLANE_STEP, Z, Z_STEP, XY, XY_STEP, KINDS = range(11)

Z_ORDER = (9, 7, 11, 8, 5, 13, 6, 10, 3, 15, 4, 12, 1, 2, 14)
XY_ORDER = (21, 13, 19, 23, 29, 20, 5, 11, 15, 17, 27, 31, 12, 18, 22, 28, 3, 7, 9, 25, 4, 10, 14, 16, 26, 30, 1, 2, 6, 8, 24)


def far_first(n):
    return 2 + n - (n // 2) * (2 * n - 1)


def add_rows(stack, row):
    for bit in (1, 2, 4):
        keep = (row & bit) == 0
        stack = [
            jnp.where(keep, u, v) + pltpu.roll(jnp.where(keep, v, u), 8 - bit, 0)
            for u, v in zip(stack[0::2], stack[1::2])
        ]
    return stack[0]


def encode(value):
    top = jnp.maximum(jnp.max(value, axis=0, keepdims=True), 2e-34)
    codes = (value * (STEPS / top) + 0.5).astype(jnp.int32) - OFFSET
    return codes.astype(jnp.int16), top * (1.0 / STEPS)


def decode(codes, step):
    return (codes.astype(jnp.int32).astype(jnp.float32) + OFFSET) * step


def split(value):
    high = value.astype(jnp.bfloat16)
    return high, (value - high.astype(jnp.float32)).astype(jnp.bfloat16)


def kernel(
    t_hbm, b_hbm, ct_hbm, a_hbm, restart_hbm, up_ref, gram_ref,
    t_ref, prod, b_in, ct_in, a_in, flags,
    b_slots, b_block, b_all, ct_all, weight_c,
    give, got, mine, out_rs, in_rs, out_step, in_step, weight_g, coef,
    gram_out, gram_z, gram_half, gram_xy,
    gram_step, gram_z_step, half_step, gram_xy_step,
    t_sem, in_sem, core_r, sent, got_all,
):
    f32, bf16 = jnp.float32, jnp.bfloat16
    ia, ja, y = lax.axis_index("ia"), lax.axis_index("ja"), lax.axis_index("ka")
    z_lo, x, z_hi, core = ia // 4, ia % 4, ja // 2, ja % 2
    z = z_hi * 2 + z_lo

    def device(z, x, y, core):
        return ((z % 2) * 4 + x, (z // 2) * 2 + core, y)

    def remote(src, dst, send, recv, to):
        return pltpu.make_async_remote_copy(
            src_ref=src, dst_ref=dst, send_sem=send, recv_sem=recv, device_id=to, device_id_type=MESH
        )

    def exchange(ref, kind):
        return remote(ref, ref, sent.at[kind], got_all.at[kind], device(z, x, y, 1 - core))

    loads = [
        pltpu.make_async_copy(b_hbm, b_in, in_sem.at[0]),
        pltpu.make_async_copy(ct_hbm, ct_in, in_sem.at[1]),
        pltpu.make_async_copy(a_hbm, a_in, in_sem.at[2]),
        pltpu.make_async_copy(restart_hbm, flags, in_sem.at[3]),
    ]
    for load in loads:
        load.start()

    def tensor_load(n):
        rows = pl.ds(n * GROUP * 64, GROUP * 64)
        return pltpu.make_async_copy(t_hbm.at[rows], t_ref.at[rows], t_sem.at[n])

    for n in range(BLOCKS // GROUP):
        tensor_load(n).start(priority=n % 2)

    barrier = pltpu.get_barrier_semaphore()

    def greet(to):
        pl.semaphore_signal(barrier, inc=1, device_id=to, device_id_type=MESH)

    @pl.loop(1, 32)
    def _(n):
        greet(device((z + 2 * (n // 8)) % 8, x, (y + (n // 2) % 4) % 4, (core + n % 2) % 2))

    @pl.loop(0, 8)
    def _(n):
        greet(device((z + 1 + 2 * (n // 2)) % 8, x, y, n % 2))

    @pl.loop(0, 24)
    def _(n):
        greet(device(z, (x + 1 + n // 8) % 4, (n // 2) % 4, n % 2))

    for load in loads:
        load.wait()
    ct = ct_in[...]
    wide_c = ct.astype(f32).T.astype(bf16)
    zero = jnp.zeros((128, 64), bf16)
    weight_c[...] = jnp.concatenate(
        [jnp.concatenate([wide_c, zero], 1), jnp.concatenate([zero, wide_c], 1)], 0
    )
    ct_all[y] = jnp.concatenate([ct, ct], 0)
    b_own = b_in[...].astype(f32)
    b_slots[y, 0:4, :] = jnp.concatenate([b_own, b_own], 1)

    def product(n):
        tensor_load(n).wait()
        rows = t_ref[pl.ds(n * GROUP * 64, GROUP * 64)].reshape(GROUP, 64, 16, 128)
        left = rows[:, :HALF].reshape(GROUP * HALF * 16, 128)
        right = rows[:, HALF:].reshape(GROUP * HALF * 16, 128)
        out = jnp.dot(jnp.concatenate([left, right], 1), weight_c[...], preferred_element_type=f32)
        prod[pl.ds(n * GROUP, GROUP)] = out.reshape(GROUP, HALF * 16, 128)


    tval = jnp.ones((8, 128), f32)
    for step in range(ITERS):
        flag = flags[step].astype(f32)
        tval = flag + (1.0 - flag) * tval
        t_next = (1.0 + jnp.sqrt(1.0 + 4.0 * tval * tval)) / 2.0
        coef[step] = (tval - 1.0) / t_next
        tval = t_next

    pl.semaphore_wait(barrier, 63)

    def b_copy(n):
        to = (y + n) % 4
        return remote(b_slots.at[y], b_slots.at[y], sent.at[B], got_all.at[B], device(z, x, to, core))

    def c_copy(n):
        to = (y + n) % 4
        return remote(ct_all.at[y], ct_all.at[y], sent.at[C], got_all.at[C], device(z, x, to, core))

    for n in (2, 1, 3):
        b_copy(n).start()
    for n in (2, 1, 3):
        c_copy(n).start()

    @pl.loop(0, BLOCKS // GROUP)
    def _(n):
        product(n)

    exchange(b_slots.at[0:3], B).wait()
    for part in range(4):
        b_block[4 * part : 4 * part + 4, :] = b_slots[part, 0:4, :]
    b_all[ja] = b_block[...].astype(bf16)

    row = lax.broadcasted_iota(jnp.int32, (8, 128), 0)

    def target(n):
        return (z_hi + far_first(n // 4)) % 4, (y + far_first(n % 4)) % 4

    def block_sum(n, at_core, out):
        to_z, to_y = target(n)
        block = (to_z * 2 + at_core) * 4 + to_y
        low, high = b_block[0:8, :], b_block[8:16, :]
        for group in range(HALF // 8):
            stack = []
            for pair in range(8):
                start = (group * 8 + pair) * 16
                stack.append(
                    prod[block, start : start + 8, :] * low + prod[block, start + 8 : start + 16, :] * high
                )
            out[n, group * 8 : group * 8 + 8, :] = add_rows(stack, row)

    def core_copy(n):
        return remote(give.at[n], got.at[n], sent.at[CORE], core_r.at[n // 4], device(z, x, y, 1 - core))

    @pl.loop(0, 16)
    def _(n):
        block_sum(n, 1 - core, give)
        core_copy(n).start()

    def ball_copy(n):
        to = (ja + n) % 8
        return remote(
            b_all.at[ja], b_all.at[ja], sent.at[B_ALL], got_all.at[B_ALL], device((to // 2) * 2 + z_lo, x, y, to % 2)
        )

    for n in range(1, 8):
        ball_copy(n).start()

    @pl.loop(0, 16)
    def _(n):
        block_sum(n, core, mine)

    def plane_copy(n, src, dst, kind):
        to_z, to_y = target(n)
        return remote(src.at[n], dst.at[n], sent.at[kind], got_all.at[kind], device(to_z * 2 + z_lo, x, to_y, core))

    for part in range(4):
        blocks = got.at[4 * part : 4 * part + 4]
        remote(blocks, blocks, sent.at[CORE], core_r.at[part], device(z, x, y, 1 - core)).wait_recv()

        @pl.loop(4 * part, min(4 * part + 4, 15))
        def _(n):
            out_rs[n], out_step[n] = encode(mine[n] + got[n])
            plane_copy(n, out_rs, in_rs, PLANE).start()
            plane_copy(n, out_step, in_step, PLANE_STEP).start()

    exchange(ct_all.at[0:3], C).wait()
    exchange(b_all.at[0:7], B_ALL).wait()
    b_rows = b_all[...].reshape(128, 128)
    gram_b = lax.dot_general(b_rows, b_rows, (((0,), (0,)), ((), ())), preferred_element_type=f32)
    gram_c = jnp.zeros((128, 128), f32)
    for part in range(4):
        piece = ct_all[part]
        gram_c += lax.dot_general(piece, piece, (((1,), (1,)), ((), ())), preferred_element_type=f32)
    rows2 = lax.broadcasted_iota(jnp.int32, (128, 128), 0)
    cols2 = lax.broadcasted_iota(jnp.int32, (128, 128), 1)
    gram = jnp.where((rows2 < 64) == (cols2 < 64), gram_b * gram_c, 0.0)
    lip = jnp.sqrt(0.5 * jnp.sum(jnp.sum(gram * gram, axis=0, keepdims=True), axis=1, keepdims=True))
    high, low = split(gram / lip)
    both = jnp.concatenate([high, low], 1)
    weight_g[...] = jnp.concatenate([both, both], 0)
    inverse = 1.0 / lip

    total = mine[15] + got[15]
    exchange(in_step.at[0:15], PLANE_STEP).wait_recv()
    exchange(in_rs.at[0:15], PLANE).wait_recv()
    for n in range(15):
        total = total + decode(in_rs[n], in_step[n])
    target_term = total * inverse

    start = a_in[...]
    current = jnp.concatenate([start[:HALF], start[HALF:]], 1)

    look = current
    weights = weight_g[...]
    for step in range(ITERS):
        flag = flags[step].astype(f32)
        look = flag * current + (1.0 - flag) * look
        high, low = split(look)
        wide = jnp.dot(jnp.concatenate([high, low], 1), weights, preferred_element_type=f32)
        grad = wide[:, :128] + wide[:, 128:] - target_term
        nxt = jnp.maximum(look - grad, 0.0)
        look = nxt + coef[step, 0:1, :] * (nxt - current)
        current = nxt

    turned = pltpu.roll(current, 64, 1)
    high, low = split(jnp.concatenate([current, turned], 0))
    gram_a = lax.dot_general(
        jnp.concatenate([high, low, high], 0),
        jnp.concatenate([high, high, low], 0),
        (((0,), (0,)), ((), ())),
        preferred_element_type=f32,
    )
    lane = lax.broadcasted_iota(jnp.int32, (HALF, 128), 1)
    packed = jnp.where(lane < 64, gram_a[0:32], gram_a[96:128])
    gram_out[0], gram_step[0] = encode(packed[:16])
    gram_out[1], gram_step[1] = encode(packed[16:])

    def z_peer(n):
        step, other = divmod(Z_ORDER[n], 2)
        return (z + step) % 8, (core + other) % 2

    def z_copy(n, src, dst, kind):
        to_z, to_core = z_peer(n)
        return remote(
            src.at[to_core], dst.at[core * 8 + z], sent.at[kind], got_all.at[kind], device(to_z, x, y, to_core)
        )

    for n in range(15):
        z_copy(n, gram_out, gram_z, Z).start()
        z_copy(n, gram_step, gram_z_step, Z_STEP).start()
    gram_z[core * 8 + z] = gram_out[core]
    gram_z_step[core * 8 + z] = gram_step[core]
    up_ref[0:HALF, :] = current[:, :64]
    up_ref[HALF:, :] = current[:, 64:]
    exchange(gram_z.at[0:15], Z).wait_recv()
    exchange(gram_z_step.at[0:15], Z_STEP).wait_recv()
    half = decode(gram_z[0], gram_z_step[0])
    for n in range(1, 16):
        half = half + decode(gram_z[n], gram_z_step[n])
    gram_half[...], half_step[...] = encode(half)

    def xy_copy(n, src, dst, kind):
        step, other = divmod(XY_ORDER[n], 2)
        to_x, to_y = (x + step // 4) % 4, (y + step % 4) % 4
        to_core = (core + other) % 2
        return remote(
            src, dst.at[core * 16 + x * 4 + y], sent.at[kind], got_all.at[kind], device(z, to_x, to_y, to_core)
        )

    for n in range(31):
        xy_copy(n, gram_half, gram_xy, XY).start()
        xy_copy(n, half_step, gram_xy_step, XY_STEP).start()
    gram_xy[core * 16 + x * 4 + y] = gram_half[...]
    gram_xy_step[core * 16 + x * 4 + y] = half_step[...]
    exchange(gram_xy.at[0:31], XY).wait_recv()
    exchange(gram_xy_step.at[0:31], XY_STEP).wait_recv()
    for part in range(2):
        whole = decode(gram_xy[16 * part], gram_xy_step[16 * part])
        for n in range(1, 16):
            whole = whole + decode(gram_xy[16 * part + n], gram_xy_step[16 * part + n])
        gram_ref[16 * part : 16 * part + 16, :] = whole[:, :64]
        gram_ref[HALF + 16 * part : HALF + 16 * part + 16, :] = whole[:, 64:]

    exchange(give, CORE).wait_send()
    exchange(out_rs.at[0:15], PLANE).wait_send()
    exchange(out_step.at[0:15], PLANE_STEP).wait_send()
    exchange(gram_z.at[0:15], Z).wait_send()
    exchange(gram_z_step.at[0:15], Z_STEP).wait_send()
    exchange(gram_xy.at[0:31], XY).wait_send()
    exchange(gram_xy_step.at[0:31], XY_STEP).wait_send()


def write_out(up_ref, gram_ref, up_hbm, gram_hbm, sem):
    copies = [
        pltpu.make_async_copy(up_ref, up_hbm, sem.at[0]),
        pltpu.make_async_copy(gram_ref, gram_hbm, sem.at[1]),
    ]
    for copy in copies:
        copy.start()
    for copy in copies:
        copy.wait()


def shards(tensor, factor_b, factor_c, factor_a, restart):
    f32, bf16 = jnp.float32, jnp.bfloat16
    dma = pltpu.SemaphoreType.DMA
    result = jax.ShapeDtypeStruct((64, 64), f32)
    operands = [
        pltpu.with_memory_space_constraint(array, pltpu.HBM)
        for array in (tensor, factor_b, factor_c.T, factor_a, restart)
    ]
    updated, gram_a = pl.pallas_call(
        kernel,
        out_shape=(pltpu.VMEM((64, 64), f32), pltpu.VMEM((64, 64), f32)),
        in_specs=[pl.BlockSpec(memory_space=pltpu.HBM)] * 5,
        out_specs=[pl.BlockSpec(memory_space=pltpu.VMEM)] * 2,
        scratch_shapes=[
            pltpu.VMEM((BLOCKS * 64, 16, 128), bf16),
            pltpu.VMEM((BLOCKS, 512, 128), f32),
            pltpu.VMEM((4, 64), bf16),
            pltpu.VMEM((64, 128), bf16),
            pltpu.VMEM((64, 64), f32),
            pltpu.SMEM((ITERS,), jnp.int32),
            pltpu.VMEM((4, 8, 128), f32),
            pltpu.VMEM((16, 128), f32),
            pltpu.VMEM((8, 16, 128), bf16),
            pltpu.VMEM((4, 128, 128), bf16),
            pltpu.VMEM((256, 128), bf16),
            pltpu.VMEM((16, HALF, 128), f32),
            pltpu.VMEM((16, HALF, 128), f32),
            pltpu.VMEM((16, HALF, 128), f32),
            pltpu.VMEM((16, HALF, 128), jnp.int16),
            pltpu.VMEM((16, HALF, 128), jnp.int16),
            pltpu.VMEM((16, 1, 128), f32),
            pltpu.VMEM((16, 1, 128), f32),
            pltpu.VMEM((256, 256), bf16),
            pltpu.VMEM((ITERS, 8, 128), f32),
            pltpu.VMEM((2, 16, 128), jnp.int16),
            pltpu.VMEM((16, 16, 128), jnp.int16),
            pltpu.VMEM((16, 128), jnp.int16),
            pltpu.VMEM((32, 16, 128), jnp.int16),
            pltpu.VMEM((2, 1, 128), f32),
            pltpu.VMEM((16, 1, 128), f32),
            pltpu.VMEM((1, 128), f32),
            pltpu.VMEM((32, 1, 128), f32),
            dma((BLOCKS // GROUP,)), dma((4,)), dma((4,)), dma((KINDS,)), dma((KINDS,)),
        ],
        compiler_params=pltpu.CompilerParams(
            collective_id=0, has_side_effects=True, vmem_limit_bytes=32 * 2**20
        ),
        name="cp_update",
    )(*operands)
    return pl.pallas_call(
        write_out,
        out_shape=(result, result),
        in_specs=[pl.BlockSpec(memory_space=pltpu.VMEM)] * 2,
        out_specs=[pl.BlockSpec(memory_space=pltpu.HBM)] * 2,
        scratch_shapes=[dma((2,))],
        name="write_out",
    )(*(pltpu.with_memory_space_constraint(array, pltpu.VMEM) for array in (updated, gram_a)))


def solution(mesh):
    return jax.shard_map(
        shards,
        mesh=mesh,
        in_specs=(
            P("ia", "ja", "ka"),
            P(("ja", "ka"), None),
            P("ka", None),
            P(("ia", "ja", "ka"), None),
            P(),
        ),
        out_specs=(P(("ia", "ja", "ka"), None), P()),
        check_vma=False,
    )
```

```python
import functools

import jax
import jax.numpy as jnp
from jax import lax
from jax.experimental import pallas as pl
from jax.experimental.pallas import tpu as pltpu
from jax.sharding import PartitionSpec as P

ITERS = 12
MESH = pl.DeviceIdType.MESH
BLOCKS = 32
GROUP = 8
HALF = 32
OFFSET = 32767
STEPS = 2.0 * OFFSET
B, C, B_ALL, CORE, PLANE, PLANE_STEP, Z, Z_STEP, XY, XY_STEP, KINDS = range(11)

Z_ORDER = (9, 7, 11, 8, 5, 13, 6, 10, 3, 15, 4, 12, 1, 2, 14)
XY_ORDER = (21, 13, 19, 23, 29, 20, 5, 11, 15, 17, 27, 31, 12, 18, 22, 28, 3, 7, 9, 25, 4, 10, 14, 16, 26, 30, 1, 2, 6, 8, 24)


def far_first(n):
    return 2 + n - (n // 2) * (2 * n - 1)


def add_rows(stack, row):
    for bit in (1, 2, 4):
        keep = (row & bit) == 0
        stack = [
            jnp.where(keep, u, v) + pltpu.roll(jnp.where(keep, v, u), 8 - bit, 0)
            for u, v in zip(stack[0::2], stack[1::2])
        ]
    return stack[0]


def encode(value):
    top = jnp.maximum(jnp.max(value, axis=0, keepdims=True), 2e-34)
    codes = (value * (STEPS / top) + 0.5).astype(jnp.int32) - OFFSET
    return codes.astype(jnp.int16), top * (1.0 / STEPS)


def decode(codes, step):
    return (codes.astype(jnp.int32).astype(jnp.float32) + OFFSET) * step


def split(value):
    high = value.astype(jnp.bfloat16)
    return high, (value - high.astype(jnp.float32)).astype(jnp.bfloat16)


def kernel(
    t_hbm, b_hbm, ct_hbm, a_hbm, restart_hbm, up_ref, gram_ref,
    t_ref, prod, b_in, ct_in, a_in, flags,
    b_slots, b_block, b_all, ct_all, weight_c,
    give, got, mine, out_rs, in_rs, out_step, in_step, weight_g, coef,
    gram_out, gram_z, gram_half, gram_xy,
    gram_step, gram_z_step, half_step, gram_xy_step,
    t_sem, in_sem, core_r, sent, got_all,
):
    f32, bf16 = jnp.float32, jnp.bfloat16
    ia, ja, y = lax.axis_index("ia"), lax.axis_index("ja"), lax.axis_index("ka")
    z_lo, x, z_hi, core = ia // 4, ia % 4, ja // 2, ja % 2
    z = z_hi * 2 + z_lo

    def device(z, x, y, core):
        return ((z % 2) * 4 + x, (z // 2) * 2 + core, y)

    def remote(src, dst, send, recv, to):
        return pltpu.make_async_remote_copy(
            src_ref=src, dst_ref=dst, send_sem=send, recv_sem=recv, device_id=to, device_id_type=MESH
        )

    def exchange(ref, kind):
        return remote(ref, ref, sent.at[kind], got_all.at[kind], device(z, x, y, 1 - core))

    loads = [
        pltpu.make_async_copy(b_hbm, b_in, in_sem.at[0]),
        pltpu.make_async_copy(ct_hbm, ct_in, in_sem.at[1]),
        pltpu.make_async_copy(a_hbm, a_in, in_sem.at[2]),
        pltpu.make_async_copy(restart_hbm, flags, in_sem.at[3]),
    ]
    for load in loads:
        load.start()

    def tensor_load(n):
        rows = pl.ds(n * GROUP * 64, GROUP * 64)
        return pltpu.make_async_copy(t_hbm.at[rows], t_ref.at[rows], t_sem.at[n])

    for n in range(BLOCKS // GROUP):
        tensor_load(n).start(priority=n % 2)

    barrier = pltpu.get_barrier_semaphore()

    def greet(to):
        pl.semaphore_signal(barrier, inc=1, device_id=to, device_id_type=MESH)

    @pl.loop(0, 31)
    def _(n):
        to_z, to_y = (z + 2 * far_first(n // 8)) % 8, (y + far_first((n // 2) % 4)) % 4
        greet(device(to_z, x, to_y, (core + 1 + n % 2) % 2))

    @pl.loop(0, 8)
    def _(n):
        greet(device((z + 1 + 2 * (n // 2)) % 8, x, y, n % 2))

    @pl.loop(0, 24)
    def _(n):
        greet(device(z, (x + 1 + n // 8) % 4, (n // 2) % 4, n % 2))

    for load in loads:
        load.wait()
    ct = ct_in[...]
    wide_c = ct.astype(f32).T.astype(bf16)
    zero = jnp.zeros((128, 64), bf16)
    weight_c[...] = jnp.concatenate(
        [jnp.concatenate([wide_c, zero], 1), jnp.concatenate([zero, wide_c], 1)], 0
    )
    ct_all[y] = jnp.concatenate([ct, ct], 0)
    b_own = b_in[...].astype(f32)
    b_slots[y, 0:4, :] = jnp.concatenate([b_own, b_own], 1)

    def product(n):
        tensor_load(n).wait()
        rows = t_ref[pl.ds(n * GROUP * 64, GROUP * 64)].reshape(GROUP, 64, 16, 128)
        left = rows[:, :HALF].reshape(GROUP * HALF * 16, 128)
        right = rows[:, HALF:].reshape(GROUP * HALF * 16, 128)
        out = jnp.dot(jnp.concatenate([left, right], 1), weight_c[...], preferred_element_type=f32)
        prod[pl.ds(n * GROUP, GROUP)] = out.reshape(GROUP, HALF * 16, 128)


    tval = jnp.ones((8, 128), f32)
    for step in range(ITERS):
        flag = flags[step].astype(f32)
        tval = flag + (1.0 - flag) * tval
        t_next = (1.0 + jnp.sqrt(1.0 + 4.0 * tval * tval)) / 2.0
        coef[step] = (tval - 1.0) / t_next
        tval = t_next

    pl.semaphore_wait(barrier, 63)

    def b_copy(n):
        to = (y + n) % 4
        return remote(b_slots.at[y], b_slots.at[y], sent.at[B], got_all.at[B], device(z, x, to, core))

    def c_copy(n):
        to = (y + n) % 4
        return remote(ct_all.at[y], ct_all.at[y], sent.at[C], got_all.at[C], device(z, x, to, core))

    for n in (2, 1, 3):
        b_copy(n).start()
    for n in (2, 1, 3):
        c_copy(n).start()

    @pl.loop(0, BLOCKS // GROUP)
    def _(n):
        product(n)

    exchange(b_slots.at[0:3], B).wait()
    for part in range(4):
        b_block[4 * part : 4 * part + 4, :] = b_slots[part, 0:4, :]
    b_all[ja] = b_block[...].astype(bf16)

    row = lax.broadcasted_iota(jnp.int32, (8, 128), 0)

    def target(n):
        return (z_hi + far_first(n // 4)) % 4, (y + far_first(n % 4)) % 4

    def block_sum(n, at_core, out):
        to_z, to_y = target(n)
        block = (to_z * 2 + at_core) * 4 + to_y
        low, high = b_block[0:8, :], b_block[8:16, :]
        for group in range(HALF // 8):
            stack = []
            for pair in range(8):
                start = (group * 8 + pair) * 16
                stack.append(
                    prod[block, start : start + 8, :] * low + prod[block, start + 8 : start + 16, :] * high
                )
            out[n, group * 8 : group * 8 + 8, :] = add_rows(stack, row)

    def core_copy(n):
        return remote(give.at[n], got.at[n], sent.at[CORE], core_r.at[n // 2], device(z, x, y, 1 - core))

    @pl.loop(0, 16)
    def _(n):
        block_sum(n, 1 - core, give)
        core_copy(n).start()

    def ball_copy(n):
        to = (ja + n) % 8
        return remote(
            b_all.at[ja], b_all.at[ja], sent.at[B_ALL], got_all.at[B_ALL], device((to // 2) * 2 + z_lo, x, y, to % 2)
        )

    for n in range(1, 8):
        ball_copy(n).start()

    @pl.loop(0, 16)
    def _(n):
        block_sum(n, core, mine)

    def plane_copy(n, src, dst, kind):
        to_z, to_y = target(n)
        return remote(src.at[n], dst.at[n], sent.at[kind], got_all.at[kind], device(to_z * 2 + z_lo, x, to_y, core))

    for part in range(8):
        blocks = got.at[2 * part : 2 * part + 2]
        remote(blocks, blocks, sent.at[CORE], core_r.at[part], device(z, x, y, 1 - core)).wait_recv()

        group = range(2 * part, min(2 * part + 2, 15))
        for n in group:
            out_rs[n], out_step[n] = encode(mine[n] + got[n])
        for n in group:
            plane_copy(n, out_rs, in_rs, PLANE).start()
            plane_copy(n, out_step, in_step, PLANE_STEP).start()

    exchange(ct_all.at[0:3], C).wait()
    exchange(b_all.at[0:7], B_ALL).wait()
    b_rows = b_all[...].reshape(128, 128)
    gram_b = lax.dot_general(b_rows, b_rows, (((0,), (0,)), ((), ())), preferred_element_type=f32)
    gram_c = jnp.zeros((128, 128), f32)
    for part in range(4):
        piece = ct_all[part]
        gram_c += lax.dot_general(piece, piece, (((1,), (1,)), ((), ())), preferred_element_type=f32)
    rows2 = lax.broadcasted_iota(jnp.int32, (128, 128), 0)
    cols2 = lax.broadcasted_iota(jnp.int32, (128, 128), 1)
    gram = jnp.where((rows2 < 64) == (cols2 < 64), gram_b * gram_c, 0.0)
    lip = jnp.sqrt(0.5 * jnp.sum(jnp.sum(gram * gram, axis=0, keepdims=True), axis=1, keepdims=True))
    high, low = split(gram / lip)
    both = jnp.concatenate([high, low], 1)
    weight_g[...] = jnp.concatenate([both, both], 0)
    inverse = 1.0 / lip

    total = mine[15] + got[15]
    exchange(in_step.at[0:15], PLANE_STEP).wait_recv()
    exchange(in_rs.at[0:15], PLANE).wait_recv()
    for n in range(15):
        total = total + decode(in_rs[n], in_step[n])
    target_term = total * inverse

    start = a_in[...]
    current = jnp.concatenate([start[:HALF], start[HALF:]], 1)

    look = current
    weights = weight_g[...]
    for step in range(ITERS):
        flag = flags[step].astype(f32)
        look = flag * current + (1.0 - flag) * look
        high, low = split(look)
        wide = jnp.dot(jnp.concatenate([high, low], 1), weights, preferred_element_type=f32)
        grad = wide[:, :128] + wide[:, 128:] - target_term
        nxt = jnp.maximum(look - grad, 0.0)
        look = nxt + coef[step, 0:1, :] * (nxt - current)
        current = nxt

    turned = pltpu.roll(current, 64, 1)
    high, low = split(jnp.concatenate([current, turned], 0))
    gram_a = lax.dot_general(
        jnp.concatenate([high, low, high], 0),
        jnp.concatenate([high, high, low], 0),
        (((0,), (0,)), ((), ())),
        preferred_element_type=f32,
    )
    lane = lax.broadcasted_iota(jnp.int32, (HALF, 128), 1)
    packed = jnp.where(lane < 64, gram_a[0:32], gram_a[96:128])
    gram_out[0], gram_step[0] = encode(packed[:16])
    gram_out[1], gram_step[1] = encode(packed[16:])

    def z_peer(n):
        step, other = divmod(Z_ORDER[n], 2)
        return (z + step) % 8, (core + other) % 2

    def z_copy(n, src, dst, kind):
        to_z, to_core = z_peer(n)
        return remote(
            src.at[to_core], dst.at[core * 8 + z], sent.at[kind], got_all.at[kind], device(to_z, x, y, to_core)
        )

    for n in range(15):
        z_copy(n, gram_out, gram_z, Z).start()
        z_copy(n, gram_step, gram_z_step, Z_STEP).start()
    gram_z[core * 8 + z] = gram_out[core]
    gram_z_step[core * 8 + z] = gram_step[core]
    up_ref[0:HALF, :] = current[:, :64]
    up_ref[HALF:, :] = current[:, 64:]
    exchange(gram_z.at[0:15], Z).wait_recv()
    exchange(gram_z_step.at[0:15], Z_STEP).wait_recv()
    half = decode(gram_z[0], gram_z_step[0])
    for n in range(1, 16):
        half = half + decode(gram_z[n], gram_z_step[n])
    gram_half[...], half_step[...] = encode(half)

    def xy_copy(n, src, dst, kind):
        step, other = divmod(XY_ORDER[n], 2)
        to_x, to_y = (x + step // 4) % 4, (y + step % 4) % 4
        to_core = (core + other) % 2
        return remote(
            src, dst.at[core * 16 + x * 4 + y], sent.at[kind], got_all.at[kind], device(z, to_x, to_y, to_core)
        )

    for n in range(31):
        xy_copy(n, gram_half, gram_xy, XY).start()
        xy_copy(n, half_step, gram_xy_step, XY_STEP).start()
    gram_xy[core * 16 + x * 4 + y] = gram_half[...]
    gram_xy_step[core * 16 + x * 4 + y] = half_step[...]
    exchange(gram_xy.at[0:31], XY).wait_recv()
    exchange(gram_xy_step.at[0:31], XY_STEP).wait_recv()
    for part in range(2):
        whole = decode(gram_xy[16 * part], gram_xy_step[16 * part])
        for n in range(1, 16):
            whole = whole + decode(gram_xy[16 * part + n], gram_xy_step[16 * part + n])
        gram_ref[16 * part : 16 * part + 16, :] = whole[:, :64]
        gram_ref[HALF + 16 * part : HALF + 16 * part + 16, :] = whole[:, 64:]

    exchange(give, CORE).wait_send()
    exchange(out_rs.at[0:15], PLANE).wait_send()
    exchange(out_step.at[0:15], PLANE_STEP).wait_send()
    exchange(gram_z.at[0:15], Z).wait_send()
    exchange(gram_z_step.at[0:15], Z_STEP).wait_send()
    exchange(gram_xy.at[0:31], XY).wait_send()
    exchange(gram_xy_step.at[0:31], XY_STEP).wait_send()


def write_out(up_ref, gram_ref, up_hbm, gram_hbm, sem):
    copies = [
        pltpu.make_async_copy(up_ref, up_hbm, sem.at[0]),
        pltpu.make_async_copy(gram_ref, gram_hbm, sem.at[1]),
    ]
    for copy in copies:
        copy.start()
    for copy in copies:
        copy.wait()


def shards(tensor, factor_b, factor_c, factor_a, restart):
    f32, bf16 = jnp.float32, jnp.bfloat16
    dma = pltpu.SemaphoreType.DMA
    result = jax.ShapeDtypeStruct((64, 64), f32)
    operands = [
        pltpu.with_memory_space_constraint(array, pltpu.HBM)
        for array in (tensor, factor_b, factor_c.T, factor_a, restart)
    ]
    updated, gram_a = pl.pallas_call(
        kernel,
        out_shape=(pltpu.VMEM((64, 64), f32), pltpu.VMEM((64, 64), f32)),
        in_specs=[pl.BlockSpec(memory_space=pltpu.HBM)] * 5,
        out_specs=[pl.BlockSpec(memory_space=pltpu.VMEM)] * 2,
        scratch_shapes=[
            pltpu.VMEM((BLOCKS * 64, 16, 128), bf16),
            pltpu.VMEM((BLOCKS, 512, 128), f32),
            pltpu.VMEM((4, 64), bf16),
            pltpu.VMEM((64, 128), bf16),
            pltpu.VMEM((64, 64), f32),
            pltpu.SMEM((ITERS,), jnp.int32),
            pltpu.VMEM((4, 8, 128), f32),
            pltpu.VMEM((16, 128), f32),
            pltpu.VMEM((8, 16, 128), bf16),
            pltpu.VMEM((4, 128, 128), bf16),
            pltpu.VMEM((256, 128), bf16),
            pltpu.VMEM((16, HALF, 128), f32),
            pltpu.VMEM((16, HALF, 128), f32),
            pltpu.VMEM((16, HALF, 128), f32),
            pltpu.VMEM((16, HALF, 128), jnp.int16),
            pltpu.VMEM((16, HALF, 128), jnp.int16),
            pltpu.VMEM((16, 1, 128), f32),
            pltpu.VMEM((16, 1, 128), f32),
            pltpu.VMEM((256, 256), bf16),
            pltpu.VMEM((ITERS, 8, 128), f32),
            pltpu.VMEM((2, 16, 128), jnp.int16),
            pltpu.VMEM((16, 16, 128), jnp.int16),
            pltpu.VMEM((16, 128), jnp.int16),
            pltpu.VMEM((32, 16, 128), jnp.int16),
            pltpu.VMEM((2, 1, 128), f32),
            pltpu.VMEM((16, 1, 128), f32),
            pltpu.VMEM((1, 128), f32),
            pltpu.VMEM((32, 1, 128), f32),
            dma((BLOCKS // GROUP,)), dma((4,)), dma((8,)), dma((KINDS,)), dma((KINDS,)),
        ],
        compiler_params=pltpu.CompilerParams(
            collective_id=0, has_side_effects=True, vmem_limit_bytes=32 * 2**20
        ),
        name="cp_update",
    )(*operands)
    return pl.pallas_call(
        write_out,
        out_shape=(result, result),
        in_specs=[pl.BlockSpec(memory_space=pltpu.VMEM)] * 2,
        out_specs=[pl.BlockSpec(memory_space=pltpu.HBM)] * 2,
        scratch_shapes=[dma((2,))],
        name="write_out",
    )(*(pltpu.with_memory_space_constraint(array, pltpu.VMEM) for array in (updated, gram_a)))


def solution(mesh):
    return jax.shard_map(
        shards,
        mesh=mesh,
        in_specs=(
            P("ia", "ja", "ka"),
            P(("ja", "ka"), None),
            P("ka", None),
            P(("ia", "ja", "ka"), None),
            P(),
        ),
        out_specs=(P(("ia", "ja", "ka"), None), P()),
        check_vma=False,
    )
```
